32 devices in a mesh: fsdp: 16 (over z, y, core), grp: 2 (over x).
Axes of the slice: x: 2, y: 2, z: 4, core: 2. Of those that a mesh axis runs over, the one named last changes fastest.
Arguments:
- hidden_act: bfloat16 [2, 2048, 14336], P('grp', None, 'fsdp'), may hold values from -6 to 6
- grad_output: bfloat16 [2, 2048, 4096], P('grp', 'fsdp'), may hold values from -6 to 6
- down_weight: bfloat16 [14336, 4096], P('fsdp'), may hold values from -0.09375 to 0.09375
- proj_in: bfloat16 [14336, 64], P('fsdp'), may hold values from -0.046875 to 0.046875
- proj_out: bfloat16 [4096, 64], replicated, may hold values from -0.09375 to 0.09375
- example_ids: int32 [2, 2048], P('grp'), may hold values from 0 to 7, never falling along the last dimension, each value on 1 to 512 neighbouring positions
Outputs:
- grad_hidden: bfloat16 [2, 2048, 14336], P('grp', None, 'fsdp')
- gram: float32 [4096, 4096], P('grp', 'fsdp')
- scores: float32 [16], replicated
The draws below stay inside these ranges and needn't reach their ends.
Inputs may be any that keep to these rules, and one draw needn't show every extreme that they name: `example_ids`: never falls along a group's tokens; each of the 8 examples of a group has 1 to 512 tokens, one exactly 512.
All inputs are finite; a program needn't handle non-finite values.
Results may differ from the reference program's by a relative error of at most 0.001.
Values may be sent and summed in bfloat16 or wider, within the bound.
A program may use at most 128 MiB of HBM per device.

```python
import math
import jax
import jax.numpy as jnp
import numpy as np
from jax import lax

D = 4096
FF = 14336
PROJ = 64
TOK_GRP = 2048
EX_GRP = 8
EX_MOST = 512
GROUPS = 2


def block_levels(key, shape, pieces, low, high):
    level, own = 1.0, jax.random.fold_in(key, 6)
    for position, shards_of in pieces:
        steps = jnp.exp(jax.random.uniform(jax.random.fold_in(own, position), (shards_of,), jnp.float32, low / len(pieces), high / len(pieces)))
        level = level * jnp.repeat(steps, shape[position] // shards_of).reshape([-1 if axis == position else 1 for axis in range(len(shape))])
    return level


def split_up(number_of, total, bound, slope):
    portions = [(1 << 20) // math.isqrt(rank ** slope) + 1 for rank in range(2, number_of + 1)]
    spare, holding = total - bound - (number_of - 1), [1] * (number_of - 1)
    while spare > 0:
        movable = [i for i in range(number_of - 1) if holding[i] < bound]
        pool, budget = sum([portions[i] for i in movable]), spare
        for i in movable:
            addition = min(bound - holding[i], max(1, budget * portions[i] // pool), spare)
            holding[i] = holding[i] + addition
            spare = spare - addition
    return np.array([bound] + holding)


def ragged(rng, number_of, total, most, slope):
    if number_of == 2:
        one = jax.random.randint(rng, (), max(1, total - most), min(most, total - 1) + 1)
        return jnp.stack([one, total - one])
    tallies = jnp.asarray(split_up(number_of, total, most, slope), jnp.int32)
    couples = (number_of - 1) // 2
    donor, receiver = tallies[1:1 + 2 * couples:2], tallies[2:2 + 2 * couples:2]
    margin = jnp.minimum(donor - 1, most - receiver)
    moved = jax.random.randint(jax.random.fold_in(rng, 1), (couples,), 0, 1 << 20) % (margin + 1)
    tallies = tallies.at[1:1 + 2 * couples:2].set(donor - moved).at[2:2 + 2 * couples:2].set(receiver + moved)
    return tallies[jax.random.permutation(jax.random.fold_in(rng, 2), number_of)]


def normal_values(stream_key, shape, scale, limit, pieces=(), held_as=jnp.bfloat16):
    level = block_levels(stream_key, shape, pieces, -0.22, 0.18) if pieces else 1.0
    result = jax.random.normal(stream_key, shape, jnp.float32) * scale * level
    return jnp.minimum(jnp.maximum(result, -limit), limit).astype(held_as)


def setup_inputs(seed: int = 0) -> dict:
    streams_of = jax.random.split(jax.random.key(seed), 7)
    hidden_act = normal_values(streams_of[0], (GROUPS, TOK_GRP, FF), 1.0, 6.0, ((0, 2), (2, 16)))
    grad_output = normal_values(streams_of[1], (GROUPS, TOK_GRP, D), 1.0, 6.0, ((0, 2), (1, 16)))
    down_weight = normal_values(streams_of[2], (FF, D), D ** -0.5, 0.09375, ((0, 16),))
    proj_in = normal_values(streams_of[3], (FF, PROJ), FF ** -0.5, 0.046875, ((0, 16),))
    proj_out = normal_values(streams_of[4], (D, PROJ), D ** -0.5, 0.09375)
    example_ids = jax.vmap(lambda own: jnp.searchsorted(jnp.cumsum(ragged(own, EX_GRP, TOK_GRP, EX_MOST, 2)), jnp.arange(TOK_GRP), side="right"))(jax.random.split(streams_of[5], GROUPS)).reshape((GROUPS, TOK_GRP)).astype(jnp.int32)
    return {"hidden_act": hidden_act, "grad_output": grad_output, "down_weight": down_weight, "proj_in": proj_in, "proj_out": proj_out, "example_ids": example_ids}


def inverse_diagonal(matrix):
    lower = jnp.linalg.cholesky(matrix)
    eye = jnp.eye(matrix.shape[0], dtype=matrix.dtype)
    lower_inv = jax.scipy.linalg.solve_triangular(lower, eye, lower=True)
    return jnp.sum(lower_inv * lower_inv, axis=0)

def reference(hidden_act, grad_output, down_weight, proj_in, proj_out, example_ids):
    groups = hidden_act.shape[0]
    flat_h = hidden_act.reshape(-1, FF)
    flat_g = grad_output.reshape(-1, D)
    grad_hidden = lax.dot_general(flat_g.astype(jnp.float32), down_weight.astype(jnp.float32), (((1,), (1,)), ((), ())), preferred_element_type=jnp.float32)
    grad_hidden = grad_hidden.astype(jnp.bfloat16).reshape(hidden_act.shape)
    left = jnp.dot(flat_h.astype(jnp.float32), proj_in.astype(jnp.float32), preferred_element_type=jnp.float32).reshape(groups, TOK_GRP, PROJ)
    right = jnp.dot(flat_g.astype(jnp.float32), proj_out.astype(jnp.float32), preferred_element_type=jnp.float32).reshape(groups, TOK_GRP, PROJ)
    onehot = (example_ids[:, None, :] == jnp.arange(EX_GRP, dtype=jnp.int32)[None, :, None]).astype(jnp.float32)
    feats = jnp.einsum('get,gti,gtj->geij', onehot, left, right, precision=lax.Precision.HIGHEST)
    feats = feats.reshape(groups * EX_GRP, PROJ * PROJ) * (EX_GRP / TOK_GRP) ** 0.5
    examples = groups * EX_GRP
    gram = jnp.dot(feats.T, feats, precision=lax.Precision.HIGHEST) / examples
    kernel = jnp.dot(feats, feats.T, precision=lax.Precision.HIGHEST)
    ridge = jnp.trace(kernel) / examples
    eye = jnp.eye(examples, dtype=kernel.dtype)
    scores = 1.0 - ridge * inverse_diagonal(kernel + ridge * eye)
    return (grad_hidden, gram, scores)
```

```python
import functools

import jax
import jax.numpy as jnp
from jax import lax
from jax.experimental import pallas as pl
from jax.experimental.pallas import tpu as pltpu
from jax.sharding import PartitionSpec as P

PROJ = 64
EX_GRP = 8
LANES = 128
MESH = pl.DeviceIdType.MESH
HIGH = lax.Precision.HIGHEST
NT = (((1,), (1,)), ((), ()))
TN = (((0,), (0,)), ((), ()))


def dot(a, b, dims, precision=None):
    return lax.dot_general(a, b, dims, precision=precision, preferred_element_type=jnp.float32)


def kernel(
    n, groups, scale,
    x_hbm, w_hbm, h_hbm, pin_hbm, pout_hbm, ids_ref,
    out_ref, gram_ref, score_ref,
    gath, own, w, h, pin, pout, rts, part, red, cross, feats, flat,
    local_sem, ring_send, ring_recv, sib_send, sib_recv, own_send, own_recv,
    rt_send, rt_recv, red_send, red_recv, x_send, x_recv, f_send, f_recv,
):
    chips = n // 2
    steps = chips - 1
    half_chips = chips // 2
    rows = x_hbm.shape[0]
    half = rows // 2
    width = w_hbm.shape[0]
    chunks = part.shape[0] // n
    examples = groups * EX_GRP
    gram_rows = gram_ref.shape[0]

    me = lax.axis_index("fsdp")
    grp = lax.axis_index("grp")
    core = lax.rem(me, 2)
    chip = lax.div(me, 2)
    side = lax.rem(chip, 2)
    along = lax.div(chip, 2)
    pos = (1 - side) * along + side * (chips - 1 - along)

    def chip_at(p):
        p = lax.rem(p + chips, chips)
        back = lax.div(p, half_chips)
        return (1 - back) * (2 * p) + back * (2 * (chips - 1 - p) + 1)

    right = chip_at(pos + 1) * 2 + core
    left = chip_at(pos - 1) * 2 + core
    sibling = chip * 2 + (1 - core)

    def peer(p):
        return lax.rem(me + p, n)

    def source(p):
        return lax.rem(me + n - p, n)

    def remote(src, dst, send, recv, **where):
        return pltpu.make_async_remote_copy(
            src_ref=src, dst_ref=dst, send_sem=send, recv_sem=recv,
            device_id=where, device_id_type=MESH,
        )

    loads = [
        pltpu.make_async_copy(src, dst, local_sem.at[i])
        for i, (src, dst) in enumerate(
            ((x_hbm, own.at[0]), (pout_hbm, pout), (h_hbm, h), (pin_hbm, pin), (w_hbm, w))
        )
    ]
    for load in loads:
        load.start()

    barrier = pltpu.get_barrier_semaphore()

    def greet(p, carry):
        pl.semaphore_signal(barrier, inc=1, device_id={"fsdp": peer(p)}, device_id_type=MESH)
        return carry

    lax.fori_loop(1, n, greet, 0)
    for k in range(1, groups):
        pl.semaphore_signal(
            barrier, inc=1, device_id={"grp": lax.rem(grp + k, groups)}, device_id_type=MESH
        )
    pl.semaphore_wait(barrier, n - 1 + groups - 1)

    def first(s, way):
        part_of = s % 2 if way == 0 else 1 - s % 2
        return remote(
            x_hbm.at[pl.ds(part_of * half, half)], gath.at[s, way, 0],
            ring_send.at[s, way], ring_recv.at[s, way], fsdp=right if way == 0 else left,
        )

    def onward(s, way):
        return remote(
            gath.at[s - 2, way, 0], gath.at[s, way, 0],
            ring_send.at[s, way], ring_recv.at[s, way], fsdp=right if way == 0 else left,
        )

    def across(s, way):
        return remote(
            gath.at[s, way, 0], gath.at[s, way, 1],
            sib_send.at[s, way], sib_recv.at[s, way], fsdp=sibling,
        )

    for s in range(min(2, steps)):
        for way in range(2):
            first(s, way).start()
    own_copy = remote(x_hbm, own.at[1], own_send, own_recv, fsdp=sibling)
    own_copy.start()

    def rt_copy(p):
        return remote(rts.at[me], rts.at[me], rt_send.at[p - 1], rt_recv.at[p - 1], fsdp=peer(p))

    def red_copy(p):
        return remote(
            part.at[pl.ds(peer(p) * chunks, chunks)], red.at[me],
            red_send.at[p - 1], red_recv.at[p - 1], fsdp=peer(p),
        )

    def x_copy(k):
        return remote(
            cross.at[grp], cross.at[grp], x_send.at[k - 1], x_recv.at[k - 1],
            grp=lax.rem(grp + k, groups),
        )

    def f_copy(p):
        return remote(
            feats.at[me], feats.at[me], f_send.at[p - 1], f_recv.at[p - 1], fsdp=peer(p)
        )

    def over_peers(action):
        def step(p, carry):
            action(p)
            return carry

        lax.fori_loop(1, n, step, 0)

    loads[0].wait()
    loads[1].wait()
    rts[me] = dot(pout[...], own[0], NT)
    over_peers(lambda p: rt_copy(p).start())

    def multiply(block, places):
        count = len(places)
        size = block.shape[0] // count
        for start in range(0, width, 256):
            stop = min(width, start + 256)
            product = dot(block, w[start:stop, :], NT).astype(out_ref.dtype)
            for i, place in enumerate(places):
                out_ref[pl.ds(pl.multiple_of(place, size), size), start:stop] = product[
                    i * size:(i + 1) * size
                ]

    loads[4].wait()
    own_copy.wait_recv()
    multiply(own[...].reshape(2 * rows, -1), (me * rows, sibling * rows))

    def partial_feats():
        loads[2].wait()
        loads[3].wait()
        over_peers(lambda p: rt_copy(p).wait_recv())
        r = lax.broadcasted_iota(jnp.int32, (PROJ, PROJ), 0)
        c = lax.broadcasted_iota(jnp.int32, (PROJ, PROJ), 1)
        mid = PROJ // 2
        wanted = jnp.where(r < mid, 2 * r, 2 * (r - mid) + 1)
        order = jnp.where(c == wanted, 1.0, 0.0).astype(jnp.bfloat16)
        sorted_in = lax.dot_general(
            order, pin[...], (((1,), (0,)), ((), ())), preferred_element_type=jnp.float32
        ).astype(jnp.bfloat16)
        part[...] = jnp.zeros_like(part)
        which = lax.broadcasted_iota(jnp.int32, (EX_GRP, rows), 0)
        blank = jnp.zeros((PROJ, rows), jnp.float32)

        def block(b, carry):
            piece = h[pl.ds(pl.multiple_of(b * rows, rows), rows), :]
            left_t = dot(sorted_in, piece, NT)
            onehot = jnp.where(ids_ref[b] == which, 1.0, 0.0)
            right_t = rts[b]
            total = part[...].reshape(mid * EX_GRP, LANES)
            for i, pair in enumerate(((right_t, blank), (blank, right_t))):
                rows_of = left_t[i * mid:(i + 1) * mid]
                weighted = (rows_of[:, None, :] * onehot[None]).reshape(mid * EX_GRP, rows)
                total += dot(weighted, jnp.concatenate(pair, axis=0), NT, HIGH)
            part[...] = total.reshape(part.shape)
            return carry

        lax.fori_loop(0, n, block, 0)
        over_peers(lambda p: red_copy(p).start())

    def reduce_feats():
        over_peers(lambda p: red_copy(p).wait_recv())
        total = part[pl.ds(me * chunks, chunks)]

        def add(p, total):
            return total + red[source(p)]

        cross[grp] = lax.fori_loop(1, n, add, total) * scale
        for k in range(1, groups):
            x_copy(k).start()

    def share_feats():
        for k in range(1, groups):
            x_copy(k).wait_recv()
        feats[me] = cross[...]
        over_peers(lambda p: f_copy(p).start())

    def gram_block():
        over_peers(lambda p: f_copy(p).wait_recv())
        for q in range(n):
            for m in range(chunks):
                column = (q * chunks + m) * LANES
                flat[:, column:column + LANES] = feats[q, :, m].reshape(examples, LANES)
        cols = chunks * LANES
        mine = flat[:, pl.ds(pl.multiple_of(me * cols, cols), cols)] * (1.0 / examples)
        tile = min(512, gram_rows)

        def rows_of(t, carry):
            at = pl.multiple_of(grp * gram_rows + t * tile, tile)
            gram_ref[pl.ds(pl.multiple_of(t * tile, tile), tile), :] = dot(
                flat[:, pl.ds(at, tile)], mine, TN, HIGH
            )
            return carry

        lax.fori_loop(0, gram_rows // tile, rows_of, 0)

    def score():
        every = flat[...]
        matrix = dot(every, every, NT, HIGH)
        r = lax.broadcasted_iota(jnp.int32, (examples, examples), 0)
        c = lax.broadcasted_iota(jnp.int32, (examples, examples), 1)
        diagonal = jnp.where(r == c, matrix, 0.0)
        ridge = jnp.sum(jnp.sum(diagonal, axis=1, keepdims=True), axis=0, keepdims=True)
        ridge = ridge * (1.0 / examples)
        matrix = matrix + jnp.where(r == c, ridge, 0.0)
        c1 = lax.broadcasted_iota(jnp.int32, (1, examples), 1)

        def eliminate(j, a):
            row = jnp.sum(jnp.where(r == j, a, 0.0), axis=0, keepdims=True)
            col = jnp.sum(jnp.where(c == j, a, 0.0), axis=1, keepdims=True)
            pivot = jnp.sum(jnp.where(c1 == j, row, 0.0), axis=1, keepdims=True)
            row = jnp.where(c1 == j, 1.0, row) / pivot
            return jnp.where(r == j, row, jnp.where(c == j, 0.0, a) - col * row)

        inverse = lax.fori_loop(0, examples, eliminate, matrix)
        diagonal = jnp.sum(jnp.where(r == c, inverse, 0.0), axis=0, keepdims=True)
        score_ref[...] = 1.0 - ridge * diagonal

    phases = (partial_feats, reduce_feats, share_feats, gram_block, score)

    def places(s):
        distance = lax.div(s, 2) + 1
        which = lax.rem(s, 2)
        found = []
        for way in range(2):
            at = chip_at(pos - distance if way == 0 else pos + distance)
            offset = (which if way == 0 else 1 - which) * half
            found.append((at * 2 + core) * rows + offset)
            found.append((at * 2 + 1 - core) * rows + offset)
        return found

    def finish(s):
        for way in range(2):
            across(s, way).wait_recv()
        multiply(gath[s].reshape(4 * half, -1), places(s))

    def ring(s, carry):
        for way in range(2):
            remote(
                gath.at[s, way, 0], gath.at[s, way, 0],
                ring_send.at[s, way], ring_recv.at[s, way], fsdp=right if way == 0 else left,
            ).wait_recv()

            @pl.when(s + 2 < steps)
            def _():
                onward(s + 2, way).start()

            across(s, way).start()

        for k, phase in enumerate(phases):
            pl.when(s == min(k, steps - 1))(phase)

        @pl.when(s > 0)
        def _():
            finish(s - 1)

        return carry

    lax.fori_loop(0, steps, ring, 0)
    finish(steps - 1)

    def sent(s, carry):
        for way in range(2):
            across(s, way).wait_send()

        return carry

    lax.fori_loop(0, steps, sent, 0)
    for s in range(min(2, steps)):
        for way in range(2):
            first(s, way).wait_send()

    def sent_on(s, carry):
        for way in range(2):
            onward(s, way).wait_send()
        return carry

    lax.fori_loop(2, steps, sent_on, 0)
    own_copy.wait_send()
    for copies in (rt_copy, red_copy, f_copy):
        over_peers(lambda p: copies(p).wait_send())
    for k in range(1, groups):
        x_copy(k).wait_send()


def body(hidden_act, grad_output, down_weight, proj_in, proj_out, example_ids):
    n = lax.axis_size("fsdp")
    groups = lax.axis_size("grp")
    h = hidden_act[0]
    x = grad_output[0]
    rows, depth = x.shape
    tokens, width = h.shape
    steps = n // 2 - 1
    feat_width = PROJ * PROJ
    examples = EX_GRP * groups
    chunks = feat_width // LANES // n
    scale = (EX_GRP / tokens) ** 0.5
    ids = example_ids.reshape(n, 1, rows)
    f32, bf16 = jnp.float32, jnp.bfloat16
    dma = pltpu.SemaphoreType.DMA
    vmem = pl.BlockSpec(memory_space=pltpu.VMEM)
    hbm = pl.BlockSpec(memory_space=pl.ANY)
    out, gram, scores = pl.pallas_call(
        functools.partial(kernel, n, groups, scale),
        out_shape=(
            jax.ShapeDtypeStruct((tokens, width), bf16),
            jax.ShapeDtypeStruct((feat_width // groups, feat_width // n), f32),
            jax.ShapeDtypeStruct((1, examples), f32),
        ),
        in_specs=[hbm] * 5 + [vmem],
        out_specs=(vmem, vmem, vmem),
        scratch_shapes=[
            pltpu.VMEM((steps, 2, 2, rows // 2, depth), bf16),
            pltpu.VMEM((2, rows, depth), bf16),
            pltpu.VMEM((width, depth), bf16),
            pltpu.VMEM((tokens, width), bf16),
            pltpu.VMEM((PROJ, width), bf16),
            pltpu.VMEM((PROJ, depth), bf16),
            pltpu.VMEM((n, PROJ, rows), f32),
            pltpu.VMEM((n * chunks, EX_GRP, LANES), f32),
            pltpu.VMEM((n, chunks, EX_GRP, LANES), f32),
            pltpu.VMEM((groups, chunks, EX_GRP, LANES), f32),
            pltpu.VMEM((n, groups, chunks, EX_GRP, LANES), f32),
            pltpu.VMEM((examples, feat_width), f32),
            dma((5,)),
            dma((steps, 2)),
            dma((steps, 2)),
            dma((steps, 2)),
            dma((steps, 2)),
            dma,
            dma,
            dma((n - 1,)),
            dma((n - 1,)),
            dma((n - 1,)),
            dma((n - 1,)),
            dma((max(1, groups - 1),)),
            dma((max(1, groups - 1),)),
            dma((n - 1,)),
            dma((n - 1,)),
        ],
        compiler_params=pltpu.CompilerParams(
            collective_id=0, has_side_effects=True, vmem_limit_bytes=56 * 1024 * 1024
        ),
        cost_estimate=pl.CostEstimate(
            flops=2 * tokens * depth * width, bytes_accessed=2 * width * (depth + 2 * tokens),
            transcendentals=0,
        ),
    )(x, down_weight, h, proj_in.T, proj_out.T, ids)
    return out[None], gram, scores.reshape(examples)


def solution(mesh):
    in_specs = (
        P("grp", None, "fsdp"),
        P("grp", "fsdp", None),
        P("fsdp", None),
        P("fsdp", None),
        P(),
        P("grp", None),
    )
    out_specs = (P("grp", None, "fsdp"), P("grp", "fsdp"), P())
    return jax.shard_map(body, mesh=mesh, in_specs=in_specs, out_specs=out_specs, check_vma=False)
```

```python
import functools

import jax
import jax.numpy as jnp
from jax import lax
from jax.experimental import pallas as pl
from jax.experimental.pallas import tpu as pltpu
from jax.sharding import PartitionSpec as P

PROJ = 64
EX_GRP = 8
LANES = 128
MESH = pl.DeviceIdType.MESH
HIGH = lax.Precision.HIGHEST
NT = (((1,), (1,)), ((), ()))
TN = (((0,), (0,)), ((), ()))


def dot(a, b, dims, precision=None):
    return lax.dot_general(a, b, dims, precision=precision, preferred_element_type=jnp.float32)


def kernel(
    n, groups, scale,
    x_hbm, w_hbm, h_hbm, pin_hbm, pout_hbm, ids_ref,
    out_hbm, gram_hbm, score_ref,
    gath, own, w, h, pin, pout, rts, part, other, red, feats, flat, out, gram,
    local_sem, out_sem, gram_sem, ring_send, ring_recv, sib_send, sib_recv,
    relay_send, relay_recv,
    rt_send, rt_recv, red_send, red_recv, x_send, x_recv, f_send, f_recv,
):
    chips = n // 2
    steps = chips - 1
    half_chips = chips // 2
    rows = x_hbm.shape[0]
    half = rows // 2
    width = w_hbm.shape[0]
    chunks = part.shape[2]
    examples = groups * EX_GRP
    gram_rows = gram.shape[0]

    me = lax.axis_index("fsdp")
    grp = lax.axis_index("grp")
    core = lax.rem(me, 2)
    chip = lax.div(me, 2)
    side = lax.rem(chip, 2)
    along = lax.div(chip, 2)
    pos = (1 - side) * along + side * (chips - 1 - along)

    def chip_at(p):
        p = lax.rem(p + chips, chips)
        back = lax.div(p, half_chips)
        return (1 - back) * (2 * p) + back * (2 * (chips - 1 - p) + 1)

    right = chip_at(pos + 1) * 2 + core
    left = chip_at(pos - 1) * 2 + core
    sibling = chip * 2 + (1 - core)

    def chip_on(p):
        return lax.rem(chip + p, chips)

    def peer(p):
        return chip_on(p) * 2 + core

    def remote(src, dst, send, recv, **where):
        return pltpu.make_async_remote_copy(
            src_ref=src, dst_ref=dst, send_sem=send, recv_sem=recv,
            device_id=where, device_id_type=MESH,
        )

    loads = [
        pltpu.make_async_copy(src, dst, local_sem.at[i])
        for i, (src, dst) in enumerate(
            ((x_hbm, own.at[0]), (pout_hbm, pout), (h_hbm, h), (pin_hbm, pin), (w_hbm, w))
        )
    ]
    for load in loads:
        load.start()

    barrier = pltpu.get_barrier_semaphore()

    def greet(p, carry):
        pl.semaphore_signal(barrier, inc=1, device_id={"fsdp": peer(p)}, device_id_type=MESH)
        return carry

    lax.fori_loop(1, chips, greet, 0)
    pl.semaphore_signal(barrier, inc=1, device_id={"fsdp": sibling}, device_id_type=MESH)
    for k in range(1, groups):
        pl.semaphore_signal(
            barrier, inc=1, device_id={"grp": lax.rem(grp + k, groups)}, device_id_type=MESH
        )
    pl.semaphore_wait(barrier, chips + groups - 1)

    def first(s, way):
        part_of = s % 2 if way == 0 else 1 - s % 2
        return remote(
            x_hbm.at[pl.ds(part_of * half, half)], gath.at[s, way, 0],
            ring_send.at[s, way], ring_recv.at[s, way], fsdp=right if way == 0 else left,
        )

    def onward(s, way):
        return remote(
            gath.at[s - 2, way, 0], gath.at[s, way, 0],
            ring_send.at[s, way], ring_recv.at[s, way], fsdp=right if way == 0 else left,
        )

    def across(s, way):
        return remote(
            gath.at[s, way, 0], gath.at[s, way, 1],
            sib_send.at[s, way], sib_recv.at[s, way], fsdp=sibling,
        )

    for s in range(min(2, steps)):
        for way in range(2):
            first(s, way).start()
    def relay(i, src, dst):
        return remote(src, dst, relay_send.at[i], relay_recv.at[i], fsdp=sibling)

    own_copy = relay(0, x_hbm, own.at[1])
    rt_relay = relay(1, rts.at[core], rts.at[core])
    part_relay = relay(2, part.at[1 - core], other)
    feats_relay = relay(3, feats.at[grp, core], feats.at[grp, core])
    own_copy.start()

    def rt_copy(p):
        mine = rts.at[core, chip]
        return remote(mine, mine, rt_send.at[p - 1], rt_recv.at[p - 1], fsdp=peer(p))

    def red_copy(p):
        return remote(
            part.at[core, chip_on(p)], red.at[chip],
            red_send.at[p - 1], red_recv.at[p - 1], fsdp=peer(p),
        )

    def f_copy(p):
        mine = feats.at[grp, core, chip]
        return remote(mine, mine, f_send.at[p - 1], f_recv.at[p - 1], fsdp=peer(p))

    def x_copy(k):
        return remote(
            feats.at[grp], feats.at[grp], x_send.at[k - 1], x_recv.at[k - 1],
            grp=lax.rem(grp + k, groups),
        )

    def over_peers(action):
        def step(p, carry):
            action(p)
            return carry

        lax.fori_loop(1, chips, step, 0)

    loads[0].wait()
    loads[1].wait()
    rts[core, chip] = dot(pout[...], own[0], NT)
    over_peers(lambda p: rt_copy(p).start())

    def out_copies(unit, places):
        return [
            pltpu.make_async_copy(
                out.at[unit, pl.ds(i * half, half)],
                out_hbm.at[pl.ds(pl.multiple_of(place, half), half)],
                out_sem.at[unit, i],
            )
            for i, place in enumerate(places)
        ]

    def multiply(unit, block, places):
        for start in range(0, width, 256):
            stop = min(width, start + 256)
            out[unit, :, start:stop] = dot(block, w[start:stop, :], NT).astype(out.dtype)
        for copy in out_copies(unit, places):
            copy.start()

    loads[4].wait()
    own_copy.wait_recv()
    own_places = (me * rows, me * rows + half, sibling * rows, sibling * rows + half)
    multiply(0, own[...].reshape(2 * rows, -1), own_places)
    over_peers(lambda p: rt_copy(p).wait_recv())
    rt_relay.start()

    def partial_feats():
        loads[2].wait()
        loads[3].wait()
        rt_relay.wait_recv()
        r = lax.broadcasted_iota(jnp.int32, (PROJ, PROJ), 0)
        c = lax.broadcasted_iota(jnp.int32, (PROJ, PROJ), 1)
        mid = PROJ // 2
        odd = lax.div(r, mid)
        spot = lax.rem(r, mid)
        holder = 2 * lax.div(lax.rem(spot, mid // 2), chunks) + lax.div(spot, mid // 2)
        wanted = 2 * (holder * chunks + lax.rem(spot, chunks)) + odd
        order = jnp.where(c == wanted, 1.0, 0.0).astype(jnp.bfloat16)
        sorted_in = lax.dot_general(
            order, pin[...], (((1,), (0,)), ((), ())), preferred_element_type=jnp.float32
        ).astype(jnp.bfloat16)
        part[...] = jnp.zeros_like(part)
        which = lax.broadcasted_iota(jnp.int32, (EX_GRP, rows), 0)
        blank = jnp.zeros((PROJ, rows), jnp.float32)

        def block(b, carry):
            piece = h[pl.ds(pl.multiple_of(b * rows, rows), rows), :]
            left_t = dot(sorted_in, piece, NT)
            onehot = jnp.where(ids_ref[b] == which, 1.0, 0.0)
            right_t = rts[lax.rem(b, 2), lax.div(b, 2)]
            total = part[...].reshape(mid * EX_GRP, LANES)
            for i, pair in enumerate(((right_t, blank), (blank, right_t))):
                rows_of = left_t[i * mid:(i + 1) * mid]
                weighted = (rows_of[:, None, :] * onehot[None]).reshape(mid * EX_GRP, rows)
                total += dot(weighted, jnp.concatenate(pair, axis=0), NT, HIGH)
            part[...] = total.reshape(part.shape)
            return carry

        lax.fori_loop(0, n, block, 0)
        part_relay.start()

    def reduce_chip():
        part_relay.wait_recv()
        part[core] = part[core] + other[...]
        over_peers(lambda p: red_copy(p).start())

    def reduce_feats():
        over_peers(lambda p: red_copy(p).wait_recv())

        def add(p, total):
            return total + red[lax.rem(chip + chips - p, chips)]

        feats[grp, core, chip] = lax.fori_loop(1, chips, add, part[core, chip]) * scale
        over_peers(lambda p: f_copy(p).start())

    def share_chip():
        over_peers(lambda p: f_copy(p).wait_recv())
        feats_relay.start()

    def share_groups():
        feats_relay.wait_recv()
        for k in range(1, groups):
            x_copy(k).start()

    gram_copy = pltpu.make_async_copy(gram, gram_hbm, gram_sem)

    def gram_block():
        for k in range(1, groups):
            x_copy(k).wait_recv()
        for q in range(n):
            for m in range(chunks):
                column = (q * chunks + m) * LANES
                piece = feats[:, q % 2, q // 2, m].reshape(examples, LANES)
                flat[:, column:column + LANES] = piece
        cols = chunks * LANES
        mine = flat[:, pl.ds(pl.multiple_of(me * cols, cols), cols)] * (1.0 / examples)
        tile = min(512, gram_rows)

        def rows_of(t, carry):
            at = pl.multiple_of(grp * gram_rows + t * tile, tile)
            gram[pl.ds(pl.multiple_of(t * tile, tile), tile), :] = dot(
                flat[:, pl.ds(at, tile)], mine, TN, HIGH
            )
            return carry

        lax.fori_loop(0, gram_rows // tile, rows_of, 0)
        gram_copy.start()

    def score():
        every = flat[...]
        matrix = dot(every, every, NT, HIGH)
        r = lax.broadcasted_iota(jnp.int32, (examples, examples), 0)
        c = lax.broadcasted_iota(jnp.int32, (examples, examples), 1)
        diagonal = jnp.where(r == c, matrix, 0.0)
        ridge = jnp.sum(jnp.sum(diagonal, axis=1, keepdims=True), axis=0, keepdims=True)
        ridge = ridge * (1.0 / examples)
        matrix = matrix + jnp.where(r == c, ridge, 0.0)
        c1 = lax.broadcasted_iota(jnp.int32, (1, examples), 1)

        def eliminate(j, a):
            row = jnp.sum(jnp.where(r == j, a, 0.0), axis=0, keepdims=True)
            col = jnp.sum(jnp.where(c == j, a, 0.0), axis=1, keepdims=True)
            pivot = jnp.sum(jnp.where(c1 == j, row, 0.0), axis=1, keepdims=True)
            row = jnp.where(c1 == j, 1.0, row) / pivot
            return jnp.where(r == j, row, jnp.where(c == j, 0.0, a) - col * row)

        inverse = lax.fori_loop(0, examples, eliminate, matrix)
        diagonal = jnp.sum(jnp.where(r == c, inverse, 0.0), axis=0, keepdims=True)
        score_ref[...] = 1.0 - ridge * diagonal

    phases = (
        (0, True, partial_feats), (1, True, reduce_chip), (1, False, reduce_feats),
        (2, False, share_chip), (3, True, share_groups), (4, True, gram_block), (5, True, score),
    )

    def run_phases(s, early):
        for at, when, phase in phases:
            if steps > 5:
                if when == early:
                    pl.when(s == at)(phase)
            elif early:
                pl.when(s == min(at, steps - 1))(phase)

    def places(s):
        distance = lax.div(s, 2) + 1
        which = lax.rem(s, 2)
        found = []
        for way in range(2):
            at = chip_at(pos - distance if way == 0 else pos + distance)
            offset = (which if way == 0 else 1 - which) * half
            found.append((at * 2 + core) * rows + offset)
            found.append((at * 2 + 1 - core) * rows + offset)
        return found

    def finish(s):
        for way in range(2):
            across(s, way).wait_recv()
        multiply(s + 1, gath[s].reshape(4 * half, -1), places(s))

    def ring(s, carry):
        for way in range(2):
            remote(
                gath.at[s, way, 0], gath.at[s, way, 0],
                ring_send.at[s, way], ring_recv.at[s, way], fsdp=right if way == 0 else left,
            ).wait_recv()

            @pl.when(s + 2 < steps)
            def _():
                onward(s + 2, way).start()

            across(s, way).start()

        run_phases(s, True)

        @pl.when(s > 0)
        def _():
            finish(s - 1)

        run_phases(s, False)
        return carry

    lax.fori_loop(0, steps, ring, 0)
    finish(steps - 1)

    def sent(s, carry):
        for way in range(2):
            across(s, way).wait_send()

        return carry

    lax.fori_loop(0, steps, sent, 0)
    for s in range(min(2, steps)):
        for way in range(2):
            first(s, way).wait_send()

    def sent_on(s, carry):
        for way in range(2):
            onward(s, way).wait_send()
        return carry

    lax.fori_loop(2, steps, sent_on, 0)
    for copy in (own_copy, rt_relay, part_relay, feats_relay):
        copy.wait_send()
    for copies in (rt_copy, red_copy, f_copy):
        over_peers(lambda p: copies(p).wait_send())
    for k in range(1, groups):
        x_copy(k).wait_send()
    gram_copy.wait()
    for copy in out_copies(0, own_places):
        copy.wait()

    def written(s, carry):
        for copy in out_copies(s + 1, places(s)):
            copy.wait()
        return carry

    lax.fori_loop(0, steps, written, 0)


def body(hidden_act, grad_output, down_weight, proj_in, proj_out, example_ids):
    n = lax.axis_size("fsdp")
    groups = lax.axis_size("grp")
    h = hidden_act[0]
    x = grad_output[0]
    rows, depth = x.shape
    tokens, width = h.shape
    chips = n // 2
    steps = chips - 1
    feat_width = PROJ * PROJ
    examples = EX_GRP * groups
    chunks = feat_width // LANES // n
    scale = (EX_GRP / tokens) ** 0.5
    ids = example_ids.reshape(n, 1, rows)
    f32, bf16 = jnp.float32, jnp.bfloat16
    dma = pltpu.SemaphoreType.DMA
    vmem = pl.BlockSpec(memory_space=pltpu.VMEM)
    hbm = pl.BlockSpec(memory_space=pl.ANY)
    out, gram, scores = pl.pallas_call(
        functools.partial(kernel, n, groups, scale),
        out_shape=(
            jax.ShapeDtypeStruct((tokens, width), bf16),
            jax.ShapeDtypeStruct((feat_width // groups, feat_width // n), f32),
            jax.ShapeDtypeStruct((1, examples), f32),
        ),
        in_specs=[hbm] * 5 + [vmem],
        out_specs=(hbm, hbm, vmem),
        scratch_shapes=[
            pltpu.VMEM((steps, 2, 2, rows // 2, depth), bf16),
            pltpu.VMEM((2, rows, depth), bf16),
            pltpu.VMEM((width, depth), bf16),
            pltpu.VMEM((tokens, width), bf16),
            pltpu.VMEM((PROJ, width), bf16),
            pltpu.VMEM((PROJ, depth), bf16),
            pltpu.VMEM((2, chips, PROJ, rows), f32),
            pltpu.VMEM((2, chips, chunks, EX_GRP, LANES), f32),
            pltpu.VMEM((chips, chunks, EX_GRP, LANES), f32),
            pltpu.VMEM((chips, chunks, EX_GRP, LANES), f32),
            pltpu.VMEM((groups, 2, chips, chunks, EX_GRP, LANES), f32),
            pltpu.VMEM((examples, feat_width), f32),
            pltpu.VMEM((steps + 1, 2 * rows, width), bf16),
            pltpu.VMEM((feat_width // groups, feat_width // n), f32),
            dma((5,)),
            dma((steps + 1, 4)),
            dma,
            dma((steps, 2)),
            dma((steps, 2)),
            dma((steps, 2)),
            dma((steps, 2)),
            dma((4,)),
            dma((4,)),
            dma((chips - 1,)),
            dma((chips - 1,)),
            dma((chips - 1,)),
            dma((chips - 1,)),
            dma((max(1, groups - 1),)),
            dma((max(1, groups - 1),)),
            dma((chips - 1,)),
            dma((chips - 1,)),
        ],
        compiler_params=pltpu.CompilerParams(
            collective_id=0, has_side_effects=True, vmem_limit_bytes=44 * 1024 * 1024
        ),
        cost_estimate=pl.CostEstimate(
            flops=2 * tokens * depth * width, bytes_accessed=2 * width * (depth + 2 * tokens),
            transcendentals=0,
        ),
    )(x, down_weight, h, proj_in.T, proj_out.T, ids)
    return out[None], gram, scores.reshape(examples)


def solution(mesh):
    in_specs = (
        P("grp", None, "fsdp"),
        P("grp", "fsdp", None),
        P("fsdp", None),
        P("fsdp", None),
        P(),
        P("grp", None),
    )
    out_specs = (P("grp", None, "fsdp"), P("grp", "fsdp"), P())
    return jax.shard_map(body, mesh=mesh, in_specs=in_specs, out_specs=out_specs, check_vma=False)
```

```python
import functools

import jax
import jax.numpy as jnp
from jax import lax
from jax.experimental import pallas as pl
from jax.experimental.pallas import tpu as pltpu
from jax.sharding import PartitionSpec as P

PROJ = 64
EX_GRP = 8
LANES = 128
MESH = pl.DeviceIdType.MESH
HIGH = lax.Precision.HIGHEST
NT = (((1,), (1,)), ((), ()))
TN = (((0,), (0,)), ((), ()))


def dot(a, b, dims, precision=None):
    return lax.dot_general(a, b, dims, precision=precision, preferred_element_type=jnp.float32)


def kernel(
    n, groups, scale,
    x_hbm, w_hbm, h_hbm, pin_hbm, pout_hbm, ids_hbm,
    out_hbm, gram_hbm, score_ref,
    gath, own, w, h, pin, pout, ids, rts, part, other, red, feats, flat, out, gram,
    local_sem, out_sem, gram_sem, ring_send, ring_recv, sib_send, sib_recv,
    relay_send, relay_recv, flip_send, flip_recv,
    rt_send, rt_recv, red_send, red_recv, x_send, x_recv, f_send, f_recv,
):
    chips = n // 2
    steps = chips - 1
    half_chips = chips // 2
    rows = x_hbm.shape[0]
    half = rows // 2
    width = w_hbm.shape[0]
    chunks = part.shape[2]
    examples = groups * EX_GRP
    gram_rows = gram.shape[0]

    me = lax.axis_index("fsdp")
    grp = lax.axis_index("grp")
    core = lax.rem(me, 2)
    chip = lax.div(me, 2)
    side = lax.rem(chip, 2)
    along = lax.div(chip, 2)
    pos = (1 - side) * along + side * (chips - 1 - along)

    def chip_at(p):
        p = lax.rem(p + chips, chips)
        back = lax.div(p, half_chips)
        return (1 - back) * (2 * p) + back * (2 * (chips - 1 - p) + 1)

    right = chip_at(pos + 1) * 2 + core
    left = chip_at(pos - 1) * 2 + core
    sibling = chip * 2 + (1 - core)

    def chip_on(p):
        return lax.rem(chip + p, chips)

    def peer(p):
        return chip_on(p) * 2 + core

    def remote(src, dst, send, recv, **where):
        return pltpu.make_async_remote_copy(
            src_ref=src, dst_ref=dst, send_sem=send, recv_sem=recv,
            device_id=where, device_id_type=MESH,
        )

    loads = [
        pltpu.make_async_copy(src, dst, local_sem.at[i])
        for i, (src, dst) in enumerate(
            ((x_hbm, own.at[0]), (pout_hbm, pout), (w_hbm, w), (pin_hbm, pin), (ids_hbm, ids), (h_hbm, h))
        )
    ]
    for load in loads:
        load.start()

    barrier = pltpu.get_barrier_semaphore()

    def greet(p, carry):
        pl.semaphore_signal(barrier, inc=1, device_id={"fsdp": peer(p)}, device_id_type=MESH)
        return carry

    lax.fori_loop(1, chips, greet, 0)
    pl.semaphore_signal(barrier, inc=1, device_id={"fsdp": sibling}, device_id_type=MESH)
    for k in range(1, groups):
        pl.semaphore_signal(
            barrier, inc=1, device_id={"grp": lax.rem(grp + k, groups)}, device_id_type=MESH
        )
    loads[0].wait()
    loads[1].wait()
    rts[core, side, along] = dot(pout[...], own[0], NT)
    pl.semaphore_wait(barrier, chips + groups - 1)

    def first(s, way):
        part_of = s % 2 if way == 0 else 1 - s % 2
        return remote(
            x_hbm.at[pl.ds(part_of * half, half)], gath.at[s, way, 0],
            ring_send.at[s, way], ring_recv.at[s, way], fsdp=right if way == 0 else left,
        )

    def onward(s, way):
        return remote(
            gath.at[s - 2, way, 0], gath.at[s, way, 0],
            ring_send.at[s, way], ring_recv.at[s, way], fsdp=right if way == 0 else left,
        )

    def across(s, way):
        return remote(
            gath.at[s, way, 0], gath.at[s, way, 1],
            sib_send.at[s, way], sib_recv.at[s, way], fsdp=sibling,
        )

    def rt_copy(p):
        mine = rts.at[core, side, along]
        return remote(mine, mine, rt_send.at[p - 1], rt_recv.at[p - 1], fsdp=peer(2 * p))

    def over_line(action):
        def step(p, carry):
            action(p)
            return carry

        lax.fori_loop(1, half_chips, step, 0)

    flip = (2 * along + 1 - side) * 2 + core
    rt_flip = remote(rts.at[core, side], rts.at[core, side], flip_send, flip_recv, fsdp=flip)
    over_line(lambda p: rt_copy(p).start())
    for s in range(min(2, steps)):
        for way in range(2):
            first(s, way).start()
    def relay(i, src, dst):
        return remote(src, dst, relay_send.at[i], relay_recv.at[i], fsdp=sibling)

    own_copy = relay(0, x_hbm, own.at[1])
    rt_relay = relay(1, rts.at[core], rts.at[core])
    part_relay = relay(2, part.at[1 - core], other)
    feats_relay = relay(3, feats.at[grp, core], feats.at[grp, core])
    own_copy.start()

    def red_copy(p):
        return remote(
            part.at[core, chip_on(p)], red.at[chip],
            red_send.at[p - 1], red_recv.at[p - 1], fsdp=peer(p),
        )

    def f_copy(p):
        mine = feats.at[grp, core, chip]
        return remote(mine, mine, f_send.at[p - 1], f_recv.at[p - 1], fsdp=peer(p))

    def x_copy(k):
        return remote(
            feats.at[grp], feats.at[grp], x_send.at[k - 1], x_recv.at[k - 1],
            grp=lax.rem(grp + k, groups),
        )

    def over_peers(action):
        def step(p, carry):
            action(p)
            return carry

        lax.fori_loop(1, chips, step, 0)

    def out_copies(unit, places):
        return [
            pltpu.make_async_copy(
                out.at[unit, pl.ds(i * half, half)],
                out_hbm.at[pl.ds(pl.multiple_of(place, half), half)],
                out_sem.at[unit, i],
            )
            for i, place in enumerate(places)
        ]

    def multiply(unit, block, places):
        for start in range(0, width, 256):
            stop = min(width, start + 256)
            out[unit, :, start:stop] = dot(block, w[start:stop, :], NT).astype(out.dtype)
        for copy in out_copies(unit, places):
            copy.start()

    loads[2].wait()
    own_copy.wait_recv()
    own_places = (me * rows, me * rows + half, sibling * rows, sibling * rows + half)
    multiply(0, own[...].reshape(2 * rows, -1), own_places)
    over_line(lambda p: rt_copy(p).wait_recv())
    rt_flip.start()

    def share_right():
        rt_flip.wait_recv()
        rt_relay.start()

    def partial_feats():
        for load in loads[3:]:
            load.wait()
        rt_relay.wait_recv()
        r = lax.broadcasted_iota(jnp.int32, (PROJ, PROJ), 0)
        c = lax.broadcasted_iota(jnp.int32, (PROJ, PROJ), 1)
        mid = PROJ // 2
        odd = lax.div(r, mid)
        spot = lax.rem(r, mid)
        holder = 2 * lax.div(lax.rem(spot, mid // 2), chunks) + lax.div(spot, mid // 2)
        wanted = 2 * (holder * chunks + lax.rem(spot, chunks)) + odd
        order = jnp.where(c == wanted, 1.0, 0.0).astype(jnp.bfloat16)
        sorted_in = lax.dot_general(
            order, pin[...], (((1,), (0,)), ((), ())), preferred_element_type=jnp.float32
        ).astype(jnp.bfloat16)
        part[...] = jnp.zeros_like(part)
        which = lax.broadcasted_iota(jnp.int32, (EX_GRP, rows), 0)
        blank = jnp.zeros((PROJ, rows), jnp.bfloat16)

        def halves(a):
            high = a.astype(jnp.bfloat16)
            return high, (a - high.astype(jnp.float32)).astype(jnp.bfloat16)

        def block(b, carry):
            piece = h[pl.ds(pl.multiple_of(b * rows, rows), rows), :]
            left_t = dot(sorted_in, piece, NT)
            onehot = jnp.where(ids[b] == which, 1.0, 0.0)
            right_high, right_low = halves(
                rts[lax.rem(b, 2), lax.rem(lax.div(b, 2), 2), lax.div(b, 4)]
            )
            total = part[...].reshape(mid * EX_GRP, LANES)
            for i in range(2):
                rows_of = left_t[i * mid:(i + 1) * mid]
                weighted = (rows_of[:, None, :] * onehot[None]).reshape(mid * EX_GRP, rows)
                high, low = halves(weighted)
                for a, r in ((high, right_high), (high, right_low), (low, right_high)):
                    pair = (blank, r) if i else (r, blank)
                    total += dot(a, jnp.concatenate(pair, axis=0), NT)
            part[...] = total.reshape(part.shape)
            return carry

        lax.fori_loop(0, n, block, 0)
        part_relay.start()

    def reduce_chip():
        part_relay.wait_recv()
        part[core] = part[core] + other[...]
        over_peers(lambda p: red_copy(p).start())

    def reduce_feats():
        over_peers(lambda p: red_copy(p).wait_recv())

        def add(p, total):
            return total + red[lax.rem(chip + chips - p, chips)]

        feats[grp, core, chip] = lax.fori_loop(1, chips, add, part[core, chip]) * scale
        over_peers(lambda p: f_copy(p).start())

    def share_chip():
        over_peers(lambda p: f_copy(p).wait_recv())
        feats_relay.start()

    def share_groups():
        feats_relay.wait_recv()
        for k in range(1, groups):
            x_copy(k).start()

    gram_copy = pltpu.make_async_copy(gram, gram_hbm, gram_sem)

    def gram_block():
        for k in range(1, groups):
            x_copy(k).wait_recv()
        for q in range(n):
            for m in range(chunks):
                column = (q * chunks + m) * LANES
                piece = feats[:, q % 2, q // 2, m].reshape(examples, LANES)
                flat[:, column:column + LANES] = piece
        cols = chunks * LANES
        mine = flat[:, pl.ds(pl.multiple_of(me * cols, cols), cols)] * (1.0 / examples)
        tile = min(512, gram_rows)

        def rows_of(t, carry):
            at = pl.multiple_of(grp * gram_rows + t * tile, tile)
            gram[pl.ds(pl.multiple_of(t * tile, tile), tile), :] = dot(
                flat[:, pl.ds(at, tile)], mine, TN, HIGH
            )
            return carry

        lax.fori_loop(0, gram_rows // tile, rows_of, 0)
        gram_copy.start()

    def score():
        every = flat[...]
        matrix = dot(every, every, NT, HIGH)
        r = lax.broadcasted_iota(jnp.int32, (examples, examples), 0)
        c = lax.broadcasted_iota(jnp.int32, (examples, examples), 1)
        diagonal = jnp.where(r == c, matrix, 0.0)
        ridge = jnp.sum(jnp.sum(diagonal, axis=1, keepdims=True), axis=0, keepdims=True)
        ridge = ridge * (1.0 / examples)
        matrix = matrix + jnp.where(r == c, ridge, 0.0)
        c1 = lax.broadcasted_iota(jnp.int32, (1, examples), 1)

        def eliminate(j, a):
            row = jnp.sum(jnp.where(r == j, a, 0.0), axis=0, keepdims=True)
            col = jnp.sum(jnp.where(c == j, a, 0.0), axis=1, keepdims=True)
            pivot = jnp.sum(jnp.where(c1 == j, row, 0.0), axis=1, keepdims=True)
            row = jnp.where(c1 == j, 1.0, row) / pivot
            return jnp.where(r == j, row, jnp.where(c == j, 0.0, a) - col * row)

        inverse = lax.fori_loop(0, examples, eliminate, matrix)
        diagonal = jnp.sum(jnp.where(r == c, inverse, 0.0), axis=0, keepdims=True)
        score_ref[...] = 1.0 - ridge * diagonal

    phases = (
        (0, False, share_right), (1, True, partial_feats), (1, False, reduce_chip),
        (2, False, reduce_feats), (3, False, share_chip), (4, True, share_groups),
        (4, False, gram_block), (5, False, score),
    )

    def run_phases(s, early):
        for at, when, phase in phases:
            if steps > 5:
                if when == early:
                    pl.when(s == at)(phase)
            elif early:
                pl.when(s == min(at, steps - 1))(phase)

    def places(s):
        distance = lax.div(s, 2) + 1
        which = lax.rem(s, 2)
        found = []
        for way in range(2):
            at = chip_at(pos - distance if way == 0 else pos + distance)
            offset = (which if way == 0 else 1 - which) * half
            found.append((at * 2 + core) * rows + offset)
            found.append((at * 2 + 1 - core) * rows + offset)
        return found

    def finish(s):
        for way in range(2):
            across(s, way).wait_recv()
        multiply(s + 1, gath[s].reshape(4 * half, -1), places(s))

    def ring(s, carry):
        for way in range(2):
            remote(
                gath.at[s, way, 0], gath.at[s, way, 0],
                ring_send.at[s, way], ring_recv.at[s, way], fsdp=right if way == 0 else left,
            ).wait_recv()

            @pl.when(s + 2 < steps)
            def _():
                onward(s + 2, way).start()

            across(s, way).start()

        run_phases(s, True)
        finish(s)
        run_phases(s, False)
        return carry

    lax.fori_loop(0, steps, ring, 0)

    def sent(s, carry):
        for way in range(2):
            across(s, way).wait_send()

        return carry

    lax.fori_loop(0, steps, sent, 0)
    for s in range(min(2, steps)):
        for way in range(2):
            first(s, way).wait_send()

    def sent_on(s, carry):
        for way in range(2):
            onward(s, way).wait_send()
        return carry

    lax.fori_loop(2, steps, sent_on, 0)
    for copy in (own_copy, rt_flip, rt_relay, part_relay, feats_relay):
        copy.wait_send()
    over_line(lambda p: rt_copy(p).wait_send())
    for copies in (red_copy, f_copy):
        over_peers(lambda p: copies(p).wait_send())
    for k in range(1, groups):
        x_copy(k).wait_send()
    gram_copy.wait()
    for copy in out_copies(0, own_places):
        copy.wait()

    def written(s, carry):
        for copy in out_copies(s + 1, places(s)):
            copy.wait()
        return carry

    lax.fori_loop(0, steps, written, 0)


def body(hidden_act, grad_output, down_weight, proj_in, proj_out, example_ids):
    n = lax.axis_size("fsdp")
    groups = lax.axis_size("grp")
    h = hidden_act[0]
    x = grad_output[0]
    rows, depth = x.shape
    tokens, width = h.shape
    chips = n // 2
    half_chips = chips // 2
    steps = chips - 1
    feat_width = PROJ * PROJ
    examples = EX_GRP * groups
    chunks = feat_width // LANES // n
    scale = (EX_GRP / tokens) ** 0.5
    ids = example_ids.reshape(n, 1, rows)
    f32, bf16 = jnp.float32, jnp.bfloat16
    dma = pltpu.SemaphoreType.DMA
    vmem = pl.BlockSpec(memory_space=pltpu.VMEM)
    hbm = pl.BlockSpec(memory_space=pl.ANY)
    pinned = pl.BlockSpec(memory_space=pltpu.HBM)
    out, gram, scores = pl.pallas_call(
        functools.partial(kernel, n, groups, scale),
        out_shape=(
            jax.ShapeDtypeStruct((tokens, width), bf16),
            jax.ShapeDtypeStruct((feat_width // groups, feat_width // n), f32),
            jax.ShapeDtypeStruct((1, examples), f32),
        ),
        in_specs=[pinned] * 6,
        out_specs=(hbm, hbm, vmem),
        scratch_shapes=[
            pltpu.VMEM((steps, 2, 2, rows // 2, depth), bf16),
            pltpu.VMEM((2, rows, depth), bf16),
            pltpu.VMEM((width, depth), bf16),
            pltpu.VMEM((tokens, width), bf16),
            pltpu.VMEM((PROJ, width), bf16),
            pltpu.VMEM((PROJ, depth), bf16),
            pltpu.VMEM((n, 1, rows), jnp.int32),
            pltpu.VMEM((2, 2, chips // 2, PROJ, rows), f32),
            pltpu.VMEM((2, chips, chunks, EX_GRP, LANES), f32),
            pltpu.VMEM((chips, chunks, EX_GRP, LANES), f32),
            pltpu.VMEM((chips, chunks, EX_GRP, LANES), f32),
            pltpu.VMEM((groups, 2, chips, chunks, EX_GRP, LANES), f32),
            pltpu.VMEM((examples, feat_width), f32),
            pltpu.VMEM((steps + 1, 2 * rows, width), bf16),
            pltpu.VMEM((feat_width // groups, feat_width // n), f32),
            dma((6,)),
            dma((steps + 1, 4)),
            dma,
            dma((steps, 2)),
            dma((steps, 2)),
            dma((steps, 2)),
            dma((steps, 2)),
            dma((4,)),
            dma((4,)),
            dma,
            dma,
            dma((half_chips - 1,)),
            dma((half_chips - 1,)),
            dma((chips - 1,)),
            dma((chips - 1,)),
            dma((max(1, groups - 1),)),
            dma((max(1, groups - 1),)),
            dma((chips - 1,)),
            dma((chips - 1,)),
        ],
        compiler_params=pltpu.CompilerParams(
            collective_id=0, has_side_effects=True, vmem_limit_bytes=44 * 1024 * 1024
        ),
        cost_estimate=pl.CostEstimate(
            flops=2 * tokens * depth * width, bytes_accessed=2 * width * (depth + 2 * tokens),
            transcendentals=0,
        ),
    )(x, down_weight, h, proj_in.T, proj_out.T, ids)
    return out[None], gram, scores.reshape(examples)


def solution(mesh):
    in_specs = (
        P("grp", None, "fsdp"),
        P("grp", "fsdp", None),
        P("fsdp", None),
        P("fsdp", None),
        P(),
        P("grp", None),
    )
    out_specs = (P("grp", None, "fsdp"), P("grp", "fsdp"), P())
    return jax.shard_map(body, mesh=mesh, in_specs=in_specs, out_specs=out_specs, check_vma=False)
```

```python
import functools

import jax
import jax.numpy as jnp
from jax import lax
from jax.experimental import pallas as pl
from jax.experimental.pallas import tpu as pltpu
from jax.sharding import PartitionSpec as P

PROJ = 64
EX_GRP = 8
LANES = 128
MESH = pl.DeviceIdType.MESH
HIGH = lax.Precision.HIGHEST
NT = (((1,), (1,)), ((), ()))
TN = (((0,), (0,)), ((), ()))


def dot(a, b, dims, precision=None):
    return lax.dot_general(a, b, dims, precision=precision, preferred_element_type=jnp.float32)


def kernel(
    n, groups, scale,
    x_hbm, w_hbm, h_hbm, pin_hbm, pout_hbm, ids_hbm,
    out_hbm, gram_hbm, score_ref,
    gath, own, w, h, pin, pout, ids, rts, part, other, red, feats, flat, out, gram,
    local_sem, out_sem, gram_sem, ring_send, ring_recv, sib_send, sib_recv,
    relay_send, relay_recv, flip_send, flip_recv,
    rt_send, rt_recv, red_send, red_recv, x_send, x_recv, f_send, f_recv,
):
    chips = n // 2
    steps = chips - 1
    half_chips = chips // 2
    rows = x_hbm.shape[0]
    half = rows // 2
    width = w_hbm.shape[0]
    chunks = part.shape[2]
    examples = groups * EX_GRP
    gram_rows = gram.shape[0]

    me = lax.axis_index("fsdp")
    grp = lax.axis_index("grp")
    core = lax.rem(me, 2)
    chip = lax.div(me, 2)
    side = lax.rem(chip, 2)
    along = lax.div(chip, 2)
    pos = (1 - side) * along + side * (chips - 1 - along)

    def chip_at(p):
        p = lax.rem(p + chips, chips)
        back = lax.div(p, half_chips)
        return (1 - back) * (2 * p) + back * (2 * (chips - 1 - p) + 1)

    right = chip_at(pos + 1) * 2 + core
    left = chip_at(pos - 1) * 2 + core
    sibling = chip * 2 + (1 - core)

    def chip_on(p):
        return lax.rem(chip + p, chips)

    def peer(p):
        return chip_on(p) * 2 + core

    def remote(src, dst, send, recv, **where):
        return pltpu.make_async_remote_copy(
            src_ref=src, dst_ref=dst, send_sem=send, recv_sem=recv,
            device_id=where, device_id_type=MESH,
        )

    loads = [
        pltpu.make_async_copy(src, dst, local_sem.at[i])
        for i, (src, dst) in enumerate(
            ((x_hbm, own.at[0]), (pout_hbm, pout), (w_hbm, w), (pin_hbm, pin), (ids_hbm, ids), (h_hbm, h))
        )
    ]
    for load in loads[:2]:
        load.start()

    barrier = pltpu.get_barrier_semaphore()

    def greet(p, carry):
        pl.semaphore_signal(barrier, inc=1, device_id={"fsdp": peer(p)}, device_id_type=MESH)
        return carry

    lax.fori_loop(1, chips, greet, 0)
    pl.semaphore_signal(barrier, inc=1, device_id={"fsdp": sibling}, device_id_type=MESH)
    for k in range(1, groups):
        pl.semaphore_signal(
            barrier, inc=1, device_id={"grp": lax.rem(grp + k, groups)}, device_id_type=MESH
        )
    loads[0].wait()
    loads[1].wait()
    for load in loads[2:]:
        load.start()
    rts[core, side, along] = dot(pout[...], own[0], NT)
    pl.semaphore_wait(barrier, chips + groups - 1)

    def first(s, way):
        part_of = s % 2 if way == 0 else 1 - s % 2
        return remote(
            x_hbm.at[pl.ds(part_of * half, half)], gath.at[s, way, 0],
            ring_send.at[s, way], ring_recv.at[s, way], fsdp=right if way == 0 else left,
        )

    def onward(s, way):
        return remote(
            gath.at[s - 2, way, 0], gath.at[s, way, 0],
            ring_send.at[s, way], ring_recv.at[s, way], fsdp=right if way == 0 else left,
        )

    def across(s, way):
        return remote(
            gath.at[s, way, 0], gath.at[s, way, 1],
            sib_send.at[s, way], sib_recv.at[s, way], fsdp=sibling,
        )

    def rt_copy(p):
        mine = rts.at[core, side, along]
        return remote(mine, mine, rt_send.at[p - 1], rt_recv.at[p - 1], fsdp=peer(2 * p))

    def over_line(action):
        def step(p, carry):
            action(p)
            return carry

        lax.fori_loop(1, half_chips, step, 0)

    flip = (2 * along + 1 - side) * 2 + core
    rt_flip = remote(rts.at[core, side], rts.at[core, side], flip_send, flip_recv, fsdp=flip)
    over_line(lambda p: rt_copy(p).start())
    for s in range(min(2, steps)):
        for way in range(2):
            first(s, way).start()
    def relay(i, src, dst):
        return remote(src, dst, relay_send.at[i], relay_recv.at[i], fsdp=sibling)

    own_copy = relay(0, x_hbm, own.at[1])
    rt_relay = relay(1, rts.at[core], rts.at[core])
    part_relay = relay(2, part.at[1 - core], other)
    feats_relay = relay(3, feats.at[grp, core], feats.at[grp, core])
    own_copy.start()

    def red_copy(p):
        return remote(
            part.at[core, chip_on(p)], red.at[chip],
            red_send.at[p - 1], red_recv.at[p - 1], fsdp=peer(p),
        )

    def f_copy(p):
        mine = feats.at[grp, core, chip]
        return remote(mine, mine, f_send.at[p - 1], f_recv.at[p - 1], fsdp=peer(p))

    def x_copy(k):
        return remote(
            feats.at[grp], feats.at[grp], x_send.at[k - 1], x_recv.at[k - 1],
            grp=lax.rem(grp + k, groups),
        )

    def over_peers(action):
        def step(p, carry):
            action(p)
            return carry

        lax.fori_loop(1, chips, step, 0)

    def out_copies(unit, places):
        return [
            pltpu.make_async_copy(
                out.at[unit, pl.ds(i * half, half)],
                out_hbm.at[pl.ds(pl.multiple_of(place, half), half)],
                out_sem.at[unit, i],
            )
            for i, place in enumerate(places)
        ]

    def multiply(unit, block, places):
        for start in range(0, width, 256):
            stop = min(width, start + 256)
            out[unit, :, start:stop] = dot(block, w[start:stop, :], NT).astype(out.dtype)
        for copy in out_copies(unit, places):
            copy.start()

    loads[2].wait()
    own_copy.wait_recv()
    own_places = (me * rows, me * rows + half, sibling * rows, sibling * rows + half)
    multiply(0, own[...].reshape(2 * rows, -1), own_places)
    over_line(lambda p: rt_copy(p).wait_recv())
    rt_flip.start()

    def share_right():
        rt_flip.wait_recv()
        rt_relay.start()

    def partial_feats():
        for load in loads[3:]:
            load.wait()
        rt_relay.wait_recv()
        r = lax.broadcasted_iota(jnp.int32, (PROJ, PROJ), 0)
        c = lax.broadcasted_iota(jnp.int32, (PROJ, PROJ), 1)
        mid = PROJ // 2
        odd = lax.div(r, mid)
        spot = lax.rem(r, mid)
        holder = 2 * lax.div(lax.rem(spot, mid // 2), chunks) + lax.div(spot, mid // 2)
        wanted = 2 * (holder * chunks + lax.rem(spot, chunks)) + odd
        order = jnp.where(c == wanted, 1.0, 0.0).astype(jnp.bfloat16)
        sorted_in = lax.dot_general(
            order, pin[...], (((1,), (0,)), ((), ())), preferred_element_type=jnp.float32
        ).astype(jnp.bfloat16)
        part[...] = jnp.zeros_like(part)
        which = lax.broadcasted_iota(jnp.int32, (EX_GRP, rows), 0)
        blank = jnp.zeros((PROJ, rows), jnp.bfloat16)

        def halves(a):
            high = a.astype(jnp.bfloat16)
            return high, (a - high.astype(jnp.float32)).astype(jnp.bfloat16)

        def block(b, carry):
            piece = h[pl.ds(pl.multiple_of(b * rows, rows), rows), :]
            left_t = dot(sorted_in, piece, NT)
            onehot = jnp.where(ids[b] == which, 1.0, 0.0)
            right_high, right_low = halves(
                rts[lax.rem(b, 2), lax.rem(lax.div(b, 2), 2), lax.div(b, 4)]
            )
            total = part[...].reshape(mid * EX_GRP, LANES)
            for i in range(2):
                rows_of = left_t[i * mid:(i + 1) * mid]
                weighted = (rows_of[:, None, :] * onehot[None]).reshape(mid * EX_GRP, rows)
                high, low = halves(weighted)
                for a, r in ((high, right_high), (high, right_low), (low, right_high)):
                    pair = (blank, r) if i else (r, blank)
                    total += dot(a, jnp.concatenate(pair, axis=0), NT)
            part[...] = total.reshape(part.shape)
            return carry

        lax.fori_loop(0, n, block, 0)
        part_relay.start()

    def reduce_chip():
        part_relay.wait_recv()
        part[core] = part[core] + other[...]
        over_peers(lambda p: red_copy(p).start())

    def reduce_feats():
        over_peers(lambda p: red_copy(p).wait_recv())

        def add(p, total):
            return total + red[lax.rem(chip + chips - p, chips)]

        feats[grp, core, chip] = lax.fori_loop(1, chips, add, part[core, chip]) * scale
        over_peers(lambda p: f_copy(p).start())

    def share_chip():
        over_peers(lambda p: f_copy(p).wait_recv())
        feats_relay.start()

    def share_groups():
        feats_relay.wait_recv()
        for k in range(1, groups):
            x_copy(k).start()

    gram_copy = pltpu.make_async_copy(gram, gram_hbm, gram_sem)

    def gram_block():
        for k in range(1, groups):
            x_copy(k).wait_recv()
        for q in range(n):
            for m in range(chunks):
                column = (q * chunks + m) * LANES
                piece = feats[:, q % 2, q // 2, m].reshape(examples, LANES)
                flat[:, column:column + LANES] = piece
        cols = chunks * LANES
        mine = flat[:, pl.ds(pl.multiple_of(me * cols, cols), cols)] * (1.0 / examples)
        tile = min(512, gram_rows)

        def rows_of(t, carry):
            at = pl.multiple_of(grp * gram_rows + t * tile, tile)
            gram[pl.ds(pl.multiple_of(t * tile, tile), tile), :] = dot(
                flat[:, pl.ds(at, tile)], mine, TN, HIGH
            )
            return carry

        lax.fori_loop(0, gram_rows // tile, rows_of, 0)
        gram_copy.start()

    def score():
        every = flat[...]
        matrix = dot(every, every, NT, HIGH)
        r = lax.broadcasted_iota(jnp.int32, (examples, examples), 0)
        c = lax.broadcasted_iota(jnp.int32, (examples, examples), 1)
        diagonal = jnp.where(r == c, matrix, 0.0)
        ridge = jnp.sum(jnp.sum(diagonal, axis=1, keepdims=True), axis=0, keepdims=True)
        ridge = ridge * (1.0 / examples)
        matrix = matrix + jnp.where(r == c, ridge, 0.0)
        c1 = lax.broadcasted_iota(jnp.int32, (1, examples), 1)

        def eliminate(j, a):
            row = jnp.sum(jnp.where(r == j, a, 0.0), axis=0, keepdims=True)
            col = jnp.sum(jnp.where(c == j, a, 0.0), axis=1, keepdims=True)
            pivot = jnp.sum(jnp.where(c1 == j, row, 0.0), axis=1, keepdims=True)
            row = jnp.where(c1 == j, 1.0, row) / pivot
            return jnp.where(r == j, row, jnp.where(c == j, 0.0, a) - col * row)

        inverse = lax.fori_loop(0, examples, eliminate, matrix)
        diagonal = jnp.sum(jnp.where(r == c, inverse, 0.0), axis=0, keepdims=True)
        score_ref[...] = 1.0 - ridge * diagonal

    phases = (
        (0, False, share_right), (1, True, partial_feats), (1, False, reduce_chip),
        (2, False, reduce_feats), (3, False, share_chip), (4, True, share_groups),
        (4, False, gram_block), (5, False, score),
    )

    def run_phases(s, early):
        for at, when, phase in phases:
            if steps > 5:
                if when == early:
                    pl.when(s == at)(phase)
            elif early:
                pl.when(s == min(at, steps - 1))(phase)

    def places(s):
        distance = lax.div(s, 2) + 1
        which = lax.rem(s, 2)
        found = []
        for way in range(2):
            at = chip_at(pos - distance if way == 0 else pos + distance)
            offset = (which if way == 0 else 1 - which) * half
            found.append((at * 2 + core) * rows + offset)
            found.append((at * 2 + 1 - core) * rows + offset)
        return found

    def finish(s):
        for way in range(2):
            across(s, way).wait_recv()
        multiply(s + 1, gath[s].reshape(4 * half, -1), places(s))

    def ring(s, carry):
        for way in range(2):
            remote(
                gath.at[s, way, 0], gath.at[s, way, 0],
                ring_send.at[s, way], ring_recv.at[s, way], fsdp=right if way == 0 else left,
            ).wait_recv()

            @pl.when(s + 2 < steps)
            def _():
                onward(s + 2, way).start()

            across(s, way).start()

        run_phases(s, True)
        finish(s)
        run_phases(s, False)
        return carry

    lax.fori_loop(0, steps, ring, 0)

    def sent(s, carry):
        for way in range(2):
            across(s, way).wait_send()

        return carry

    lax.fori_loop(0, steps, sent, 0)
    for s in range(min(2, steps)):
        for way in range(2):
            first(s, way).wait_send()

    def sent_on(s, carry):
        for way in range(2):
            onward(s, way).wait_send()
        return carry

    lax.fori_loop(2, steps, sent_on, 0)
    for copy in (own_copy, rt_flip, rt_relay, part_relay, feats_relay):
        copy.wait_send()
    over_line(lambda p: rt_copy(p).wait_send())
    for copies in (red_copy, f_copy):
        over_peers(lambda p: copies(p).wait_send())
    for k in range(1, groups):
        x_copy(k).wait_send()
    gram_copy.wait()
    for copy in out_copies(0, own_places):
        copy.wait()

    def written(s, carry):
        for copy in out_copies(s + 1, places(s)):
            copy.wait()
        return carry

    lax.fori_loop(0, steps, written, 0)


def body(hidden_act, grad_output, down_weight, proj_in, proj_out, example_ids):
    n = lax.axis_size("fsdp")
    groups = lax.axis_size("grp")
    h = hidden_act[0]
    x = grad_output[0]
    rows, depth = x.shape
    tokens, width = h.shape
    chips = n // 2
    half_chips = chips // 2
    steps = chips - 1
    feat_width = PROJ * PROJ
    examples = EX_GRP * groups
    chunks = feat_width // LANES // n
    scale = (EX_GRP / tokens) ** 0.5
    ids = example_ids.reshape(n, 1, rows)
    f32, bf16 = jnp.float32, jnp.bfloat16
    dma = pltpu.SemaphoreType.DMA
    vmem = pl.BlockSpec(memory_space=pltpu.VMEM)
    hbm = pl.BlockSpec(memory_space=pl.ANY)
    pinned = pl.BlockSpec(memory_space=pltpu.HBM)
    out, gram, scores = pl.pallas_call(
        functools.partial(kernel, n, groups, scale),
        out_shape=(
            jax.ShapeDtypeStruct((tokens, width), bf16),
            jax.ShapeDtypeStruct((feat_width // groups, feat_width // n), f32),
            jax.ShapeDtypeStruct((1, examples), f32),
        ),
        in_specs=[pinned] * 6,
        out_specs=(hbm, hbm, vmem),
        scratch_shapes=[
            pltpu.VMEM((steps, 2, 2, rows // 2, depth), bf16),
            pltpu.VMEM((2, rows, depth), bf16),
            pltpu.VMEM((width, depth), bf16),
            pltpu.VMEM((tokens, width), bf16),
            pltpu.VMEM((PROJ, width), bf16),
            pltpu.VMEM((PROJ, depth), bf16),
            pltpu.VMEM((n, 1, rows), jnp.int32),
            pltpu.VMEM((2, 2, chips // 2, PROJ, rows), f32),
            pltpu.VMEM((2, chips, chunks, EX_GRP, LANES), f32),
            pltpu.VMEM((chips, chunks, EX_GRP, LANES), f32),
            pltpu.VMEM((chips, chunks, EX_GRP, LANES), f32),
            pltpu.VMEM((groups, 2, chips, chunks, EX_GRP, LANES), f32),
            pltpu.VMEM((examples, feat_width), f32),
            pltpu.VMEM((steps + 1, 2 * rows, width), bf16),
            pltpu.VMEM((feat_width // groups, feat_width // n), f32),
            dma((6,)),
            dma((steps + 1, 4)),
            dma,
            dma((steps, 2)),
            dma((steps, 2)),
            dma((steps, 2)),
            dma((steps, 2)),
            dma((4,)),
            dma((4,)),
            dma,
            dma,
            dma((half_chips - 1,)),
            dma((half_chips - 1,)),
            dma((chips - 1,)),
            dma((chips - 1,)),
            dma((max(1, groups - 1),)),
            dma((max(1, groups - 1),)),
            dma((chips - 1,)),
            dma((chips - 1,)),
        ],
        compiler_params=pltpu.CompilerParams(
            collective_id=0, has_side_effects=True, vmem_limit_bytes=44 * 1024 * 1024
        ),
        cost_estimate=pl.CostEstimate(
            flops=2 * tokens * depth * width, bytes_accessed=2 * width * (depth + 2 * tokens),
            transcendentals=0,
        ),
    )(*[
        pltpu.with_memory_space_constraint(operand, pltpu.HBM)
        for operand in (x, down_weight, h, proj_in.T, proj_out.T, ids)
    ])
    return out[None], gram, scores.reshape(examples)


def solution(mesh):
    in_specs = (
        P("grp", None, "fsdp"),
        P("grp", "fsdp", None),
        P("fsdp", None),
        P("fsdp", None),
        P(),
        P("grp", None),
    )
    out_specs = (P("grp", None, "fsdp"), P("grp", "fsdp"), P())
    return jax.shard_map(body, mesh=mesh, in_specs=in_specs, out_specs=out_specs, check_vma=False)
```

```python
import functools

import jax
import jax.numpy as jnp
from jax import lax
from jax.experimental import pallas as pl
from jax.experimental.pallas import tpu as pltpu
from jax.sharding import PartitionSpec as P

PROJ = 64
EX_GRP = 8
LANES = 128
MESH = pl.DeviceIdType.MESH
HIGH = lax.Precision.HIGHEST
NT = (((1,), (1,)), ((), ()))
NN = (((1,), (0,)), ((), ()))
TN = (((0,), (0,)), ((), ()))


def dot(a, b, dims, precision=None):
    return lax.dot_general(a, b, dims, precision=precision, preferred_element_type=jnp.float32)


def kernel(
    n, groups, scale,
    x_hbm, w_hbm, h_hbm, pin_hbm, pout_hbm, ids_hbm,
    out_hbm, gram_hbm, score_ref,
    gath, own, w, h, pin, pout, ids, wt, rts, part, other, red, feats, flat, out, gram,
    local_sem, out_sem, gram_sem, ring_send, ring_recv, sib_send, sib_recv,
    relay_send, relay_recv, flip_send, flip_recv,
    rt_send, rt_recv, red_send, red_recv, x_send, x_recv, f_send, f_recv,
):
    chips = n // 2
    steps = chips - 1
    half_chips = chips // 2
    rows = x_hbm.shape[0]
    half = rows // 2
    width = w_hbm.shape[0]
    chunks = part.shape[2]
    examples = groups * EX_GRP
    gram_rows = gram.shape[0]

    me = lax.axis_index("fsdp")
    grp = lax.axis_index("grp")
    core = lax.rem(me, 2)
    chip = lax.div(me, 2)
    side = lax.rem(chip, 2)
    along = lax.div(chip, 2)
    pos = (1 - side) * along + side * (chips - 1 - along)

    def chip_at(p):
        p = lax.rem(p + chips, chips)
        back = lax.div(p, half_chips)
        return (1 - back) * (2 * p) + back * (2 * (chips - 1 - p) + 1)

    right = chip_at(pos + 1) * 2 + core
    left = chip_at(pos - 1) * 2 + core
    sibling = chip * 2 + (1 - core)

    def chip_on(p):
        return lax.rem(chip + p, chips)

    def peer(p):
        return chip_on(p) * 2 + core

    def remote(src, dst, send, recv, **where):
        return pltpu.make_async_remote_copy(
            src_ref=src, dst_ref=dst, send_sem=send, recv_sem=recv,
            device_id=where, device_id_type=MESH,
        )

    loads = [
        pltpu.make_async_copy(src, dst, local_sem.at[i])
        for i, (src, dst) in enumerate(
            ((x_hbm, own.at[0]), (pout_hbm, pout), (w_hbm, w), (pin_hbm, pin), (ids_hbm, ids), (h_hbm, h))
        )
    ]
    for load in loads[:2]:
        load.start()

    barrier = pltpu.get_barrier_semaphore()

    def greet(p, carry):
        pl.semaphore_signal(barrier, inc=1, device_id={"fsdp": peer(p)}, device_id_type=MESH)
        return carry

    lax.fori_loop(1, chips, greet, 0)
    pl.semaphore_signal(barrier, inc=1, device_id={"fsdp": sibling}, device_id_type=MESH)
    for k in range(1, groups):
        pl.semaphore_signal(
            barrier, inc=1, device_id={"grp": lax.rem(grp + k, groups)}, device_id_type=MESH
        )
    loads[0].wait()
    loads[1].wait()
    for load in loads[2:]:
        load.start()
    rts[core, side, along] = dot(pout[...], own[0], NT)
    pl.semaphore_wait(barrier, chips + groups - 1)

    def first(s, way):
        part_of = s % 2 if way == 0 else 1 - s % 2
        return remote(
            x_hbm.at[pl.ds(part_of * half, half)], gath.at[s, way, 0],
            ring_send.at[s, way], ring_recv.at[s, way], fsdp=right if way == 0 else left,
        )

    def onward(s, way):
        return remote(
            gath.at[s - 2, way, 0], gath.at[s, way, 0],
            ring_send.at[s, way], ring_recv.at[s, way], fsdp=right if way == 0 else left,
        )

    def across(s, way):
        return remote(
            gath.at[s, way, 0], gath.at[s, way, 1],
            sib_send.at[s, way], sib_recv.at[s, way], fsdp=sibling,
        )

    def rt_copy(p):
        mine = rts.at[core, side, along]
        return remote(mine, mine, rt_send.at[p - 1], rt_recv.at[p - 1], fsdp=peer(2 * p))

    def over_line(action):
        def step(p, carry):
            action(p)
            return carry

        lax.fori_loop(1, half_chips, step, 0)

    flip = (2 * along + 1 - side) * 2 + core
    rt_flip = remote(rts.at[core, side], rts.at[core, side], flip_send, flip_recv, fsdp=flip)
    over_line(lambda p: rt_copy(p).start())
    for s in range(min(2, steps)):
        for way in range(2):
            first(s, way).start()
    def relay(i, src, dst):
        return remote(src, dst, relay_send.at[i], relay_recv.at[i], fsdp=sibling)

    own_copy = relay(0, x_hbm, own.at[1])
    rt_relay = relay(1, rts.at[core], rts.at[core])
    part_relay = relay(2, part.at[1 - core], other)
    feats_relay = relay(3, feats.at[grp, core], feats.at[grp, core])
    own_copy.start()

    def red_copy(p):
        return remote(
            part.at[core, chip_on(p)], red.at[chip],
            red_send.at[p - 1], red_recv.at[p - 1], fsdp=peer(p),
        )

    def f_copy(p):
        mine = feats.at[grp, core, chip]
        return remote(mine, mine, f_send.at[p - 1], f_recv.at[p - 1], fsdp=peer(p))

    def x_copy(k):
        return remote(
            feats.at[grp], feats.at[grp], x_send.at[k - 1], x_recv.at[k - 1],
            grp=lax.rem(grp + k, groups),
        )

    def over_peers(action):
        def step(p, carry):
            action(p)
            return carry

        lax.fori_loop(1, chips, step, 0)

    def out_copies(unit, places):
        return [
            pltpu.make_async_copy(
                out.at[unit, pl.ds(i * half, half)],
                out_hbm.at[pl.ds(pl.multiple_of(place, half), half)],
                out_sem.at[unit, i],
            )
            for i, place in enumerate(places)
        ]

    def multiply(unit, block, places):
        for start in range(0, width, 256):
            stop = min(width, start + 256)
            out[unit, :, start:stop] = dot(block, wt[:, start:stop], NN).astype(out.dtype)
        for copy in out_copies(unit, places):
            copy.start()

    loads[2].wait()
    turned = min(512, w.shape[1])

    def turn(t, carry):
        at = pl.multiple_of(t * turned, turned)
        wt[pl.ds(at, turned), :] = w[:, pl.ds(at, turned)].T
        return carry

    lax.fori_loop(0, w.shape[1] // turned, turn, 0)
    own_copy.wait_recv()
    own_places = (me * rows, me * rows + half, sibling * rows, sibling * rows + half)
    multiply(0, own[...].reshape(2 * rows, -1), own_places)
    over_line(lambda p: rt_copy(p).wait_recv())
    rt_flip.start()

    def share_right():
        rt_flip.wait_recv()
        rt_relay.start()

    def partial_feats():
        for load in loads[3:]:
            load.wait()
        rt_relay.wait_recv()
        r = lax.broadcasted_iota(jnp.int32, (PROJ, PROJ), 0)
        c = lax.broadcasted_iota(jnp.int32, (PROJ, PROJ), 1)
        mid = PROJ // 2
        odd = lax.div(r, mid)
        spot = lax.rem(r, mid)
        holder = 2 * lax.div(lax.rem(spot, mid // 2), chunks) + lax.div(spot, mid // 2)
        wanted = 2 * (holder * chunks + lax.rem(spot, chunks)) + odd
        order = jnp.where(c == wanted, 1.0, 0.0).astype(jnp.bfloat16)
        sorted_in = lax.dot_general(
            order, pin[...], (((1,), (0,)), ((), ())), preferred_element_type=jnp.float32
        ).astype(jnp.bfloat16)
        part[...] = jnp.zeros_like(part)
        which = lax.broadcasted_iota(jnp.int32, (EX_GRP, rows), 0)
        blank = jnp.zeros((PROJ, rows), jnp.bfloat16)

        def halves(a):
            high = a.astype(jnp.bfloat16)
            return high, (a - high.astype(jnp.float32)).astype(jnp.bfloat16)

        def block(b, carry):
            piece = h[pl.ds(pl.multiple_of(b * rows, rows), rows), :]
            left_t = dot(sorted_in, piece, NT)
            onehot = jnp.where(ids[b] == which, 1.0, 0.0)
            right_high, right_low = halves(
                rts[lax.rem(b, 2), lax.rem(lax.div(b, 2), 2), lax.div(b, 4)]
            )
            total = part[...].reshape(mid * EX_GRP, LANES)
            for i in range(2):
                rows_of = left_t[i * mid:(i + 1) * mid]
                weighted = (rows_of[:, None, :] * onehot[None]).reshape(mid * EX_GRP, rows)
                high, low = halves(weighted)
                for a, r in ((high, right_high), (high, right_low), (low, right_high)):
                    pair = (blank, r) if i else (r, blank)
                    total += dot(a, jnp.concatenate(pair, axis=0), NT)
            part[...] = total.reshape(part.shape)
            return carry

        lax.fori_loop(0, n, block, 0)
        part_relay.start()

    def reduce_chip():
        part_relay.wait_recv()
        part[core] = part[core] + other[...]
        over_peers(lambda p: red_copy(p).start())

    def reduce_feats():
        over_peers(lambda p: red_copy(p).wait_recv())

        def add(p, total):
            return total + red[lax.rem(chip + chips - p, chips)]

        feats[grp, core, chip] = lax.fori_loop(1, chips, add, part[core, chip]) * scale
        over_peers(lambda p: f_copy(p).start())

    def share_chip():
        over_peers(lambda p: f_copy(p).wait_recv())
        feats_relay.start()

    def share_groups():
        feats_relay.wait_recv()
        for k in range(1, groups):
            x_copy(k).start()

    gram_copy = pltpu.make_async_copy(gram, gram_hbm, gram_sem)

    def gram_block():
        for k in range(1, groups):
            x_copy(k).wait_recv()
        for q in range(n):
            for m in range(chunks):
                column = (q * chunks + m) * LANES
                piece = feats[:, q % 2, q // 2, m].reshape(examples, LANES)
                flat[:, column:column + LANES] = piece
        cols = chunks * LANES
        mine = flat[:, pl.ds(pl.multiple_of(me * cols, cols), cols)] * (1.0 / examples)
        tile = min(512, gram_rows)

        def rows_of(t, carry):
            at = pl.multiple_of(grp * gram_rows + t * tile, tile)
            gram[pl.ds(pl.multiple_of(t * tile, tile), tile), :] = dot(
                flat[:, pl.ds(at, tile)], mine, TN, HIGH
            )
            return carry

        lax.fori_loop(0, gram_rows // tile, rows_of, 0)
        gram_copy.start()

    def score():
        every = flat[...]
        matrix = dot(every, every, NT, HIGH)
        r = lax.broadcasted_iota(jnp.int32, (examples, examples), 0)
        c = lax.broadcasted_iota(jnp.int32, (examples, examples), 1)
        diagonal = jnp.where(r == c, matrix, 0.0)
        ridge = jnp.sum(jnp.sum(diagonal, axis=1, keepdims=True), axis=0, keepdims=True)
        ridge = ridge * (1.0 / examples)
        matrix = matrix + jnp.where(r == c, ridge, 0.0)
        c1 = lax.broadcasted_iota(jnp.int32, (1, examples), 1)

        def eliminate(j, a):
            row = jnp.sum(jnp.where(r == j, a, 0.0), axis=0, keepdims=True)
            col = jnp.sum(jnp.where(c == j, a, 0.0), axis=1, keepdims=True)
            pivot = jnp.sum(jnp.where(c1 == j, row, 0.0), axis=1, keepdims=True)
            row = jnp.where(c1 == j, 1.0, row) / pivot
            return jnp.where(r == j, row, jnp.where(c == j, 0.0, a) - col * row)

        inverse = lax.fori_loop(0, examples, eliminate, matrix)
        diagonal = jnp.sum(jnp.where(r == c, inverse, 0.0), axis=0, keepdims=True)
        score_ref[...] = 1.0 - ridge * diagonal

    phases = (
        (0, False, share_right), (1, True, partial_feats), (1, False, reduce_chip),
        (2, False, reduce_feats), (3, False, share_chip), (4, True, share_groups),
        (4, False, gram_block), (5, False, score),
    )

    def run_phases(s, early):
        for at, when, phase in phases:
            if steps > 5:
                if when == early:
                    pl.when(s == at)(phase)
            elif early:
                pl.when(s == min(at, steps - 1))(phase)

    def places(s):
        distance = lax.div(s, 2) + 1
        which = lax.rem(s, 2)
        found = []
        for way in range(2):
            at = chip_at(pos - distance if way == 0 else pos + distance)
            offset = (which if way == 0 else 1 - which) * half
            found.append((at * 2 + core) * rows + offset)
            found.append((at * 2 + 1 - core) * rows + offset)
        return found

    def finish(s):
        for way in range(2):
            across(s, way).wait_recv()
        multiply(s + 1, gath[s].reshape(4 * half, -1), places(s))

    def ring(s, carry):
        for way in range(2):
            remote(
                gath.at[s, way, 0], gath.at[s, way, 0],
                ring_send.at[s, way], ring_recv.at[s, way], fsdp=right if way == 0 else left,
            ).wait_recv()

            @pl.when(s + 2 < steps)
            def _():
                onward(s + 2, way).start()

            across(s, way).start()

        run_phases(s, True)
        finish(s)
        run_phases(s, False)
        return carry

    lax.fori_loop(0, steps, ring, 0)

    def sent(s, carry):
        for way in range(2):
            across(s, way).wait_send()

        return carry

    lax.fori_loop(0, steps, sent, 0)
    for s in range(min(2, steps)):
        for way in range(2):
            first(s, way).wait_send()

    def sent_on(s, carry):
        for way in range(2):
            onward(s, way).wait_send()
        return carry

    lax.fori_loop(2, steps, sent_on, 0)
    for copy in (own_copy, rt_flip, rt_relay, part_relay, feats_relay):
        copy.wait_send()
    over_line(lambda p: rt_copy(p).wait_send())
    for copies in (red_copy, f_copy):
        over_peers(lambda p: copies(p).wait_send())
    for k in range(1, groups):
        x_copy(k).wait_send()
    gram_copy.wait()
    for copy in out_copies(0, own_places):
        copy.wait()

    def written(s, carry):
        for copy in out_copies(s + 1, places(s)):
            copy.wait()
        return carry

    lax.fori_loop(0, steps, written, 0)


def body(hidden_act, grad_output, down_weight, proj_in, proj_out, example_ids):
    n = lax.axis_size("fsdp")
    groups = lax.axis_size("grp")
    h = hidden_act[0]
    x = grad_output[0]
    rows, depth = x.shape
    tokens, width = h.shape
    chips = n // 2
    half_chips = chips // 2
    steps = chips - 1
    feat_width = PROJ * PROJ
    examples = EX_GRP * groups
    chunks = feat_width // LANES // n
    scale = (EX_GRP / tokens) ** 0.5
    ids = example_ids.reshape(n, 1, rows)
    f32, bf16 = jnp.float32, jnp.bfloat16
    dma = pltpu.SemaphoreType.DMA
    vmem = pl.BlockSpec(memory_space=pltpu.VMEM)
    hbm = pl.BlockSpec(memory_space=pl.ANY)
    pinned = pl.BlockSpec(memory_space=pltpu.HBM)
    out, gram, scores = pl.pallas_call(
        functools.partial(kernel, n, groups, scale),
        out_shape=(
            jax.ShapeDtypeStruct((tokens, width), bf16),
            jax.ShapeDtypeStruct((feat_width // groups, feat_width // n), f32),
            jax.ShapeDtypeStruct((1, examples), f32),
        ),
        in_specs=[pinned] * 6,
        out_specs=(hbm, hbm, vmem),
        scratch_shapes=[
            pltpu.VMEM((steps, 2, 2, rows // 2, depth), bf16),
            pltpu.VMEM((2, rows, depth), bf16),
            pltpu.VMEM((width, depth), bf16),
            pltpu.VMEM((tokens, width), bf16),
            pltpu.VMEM((PROJ, width), bf16),
            pltpu.VMEM((PROJ, depth), bf16),
            pltpu.VMEM((n, 1, rows), jnp.int32),
            pltpu.VMEM((depth, width), bf16),
            pltpu.VMEM((2, 2, chips // 2, PROJ, rows), f32),
            pltpu.VMEM((2, chips, chunks, EX_GRP, LANES), f32),
            pltpu.VMEM((chips, chunks, EX_GRP, LANES), f32),
            pltpu.VMEM((chips, chunks, EX_GRP, LANES), f32),
            pltpu.VMEM((groups, 2, chips, chunks, EX_GRP, LANES), f32),
            pltpu.VMEM((examples, feat_width), f32),
            pltpu.VMEM((steps + 1, 2 * rows, width), bf16),
            pltpu.VMEM((feat_width // groups, feat_width // n), f32),
            dma((6,)),
            dma((steps + 1, 4)),
            dma,
            dma((steps, 2)),
            dma((steps, 2)),
            dma((steps, 2)),
            dma((steps, 2)),
            dma((4,)),
            dma((4,)),
            dma,
            dma,
            dma((half_chips - 1,)),
            dma((half_chips - 1,)),
            dma((chips - 1,)),
            dma((chips - 1,)),
            dma((max(1, groups - 1),)),
            dma((max(1, groups - 1),)),
            dma((chips - 1,)),
            dma((chips - 1,)),
        ],
        compiler_params=pltpu.CompilerParams(
            collective_id=0, has_side_effects=True, vmem_limit_bytes=48 * 1024 * 1024
        ),
        cost_estimate=pl.CostEstimate(
            flops=2 * tokens * depth * width, bytes_accessed=2 * width * (depth + 2 * tokens),
            transcendentals=0,
        ),
    )(*[
        pltpu.with_memory_space_constraint(operand, pltpu.HBM)
        for operand in (x, down_weight, h, proj_in.T, proj_out.T, ids)
    ])
    return out[None], gram, scores.reshape(examples)


def solution(mesh):
    in_specs = (
        P("grp", None, "fsdp"),
        P("grp", "fsdp", None),
        P("fsdp", None),
        P("fsdp", None),
        P(),
        P("grp", None),
    )
    out_specs = (P("grp", None, "fsdp"), P("grp", "fsdp"), P())
    return jax.shard_map(body, mesh=mesh, in_specs=in_specs, out_specs=out_specs, check_vma=False)
```

```python
import functools

import jax
import jax.numpy as jnp
from jax import lax
from jax.experimental import pallas as pl
from jax.experimental.pallas import tpu as pltpu
from jax.sharding import PartitionSpec as P

PROJ = 64
EX_GRP = 8
LANES = 128
MESH = pl.DeviceIdType.MESH
HIGH = lax.Precision.HIGHEST
NT = (((1,), (1,)), ((), ()))
TN = (((0,), (0,)), ((), ()))


def dot(a, b, dims, precision=None):
    return lax.dot_general(a, b, dims, precision=precision, preferred_element_type=jnp.float32)


def kernel(
    n, groups, scale,
    x_hbm, w_hbm, h_hbm, pin_hbm, pout_hbm, ids_hbm,
    out_hbm, gram_hbm, score_ref,
    gath, own, w, h, pin, pout, ids, rts, part, other, red, feats, flat, out, gram,
    local_sem, out_sem, gram_sem, ring_send, ring_recv, sib_send, sib_recv,
    relay_send, relay_recv, flip_send, flip_recv,
    rt_send, rt_recv, red_send, red_recv, x_send, x_recv, f_send, f_recv,
):
    chips = n // 2
    steps = chips - 1
    half_chips = chips // 2
    rows = x_hbm.shape[0]
    half = rows // 2
    width = w_hbm.shape[0]
    chunks = part.shape[2]
    examples = groups * EX_GRP
    gram_rows = gram.shape[0]

    me = lax.axis_index("fsdp")
    grp = lax.axis_index("grp")
    core = lax.rem(me, 2)
    chip = lax.div(me, 2)
    side = lax.rem(chip, 2)
    along = lax.div(chip, 2)
    pos = (1 - side) * along + side * (chips - 1 - along)

    def chip_at(p):
        p = lax.rem(p + chips, chips)
        back = lax.div(p, half_chips)
        return (1 - back) * (2 * p) + back * (2 * (chips - 1 - p) + 1)

    right = chip_at(pos + 1) * 2 + core
    left = chip_at(pos - 1) * 2 + core
    sibling = chip * 2 + (1 - core)

    def chip_on(p):
        return lax.rem(chip + p, chips)

    def peer(p):
        return chip_on(p) * 2 + core

    def remote(src, dst, send, recv, **where):
        return pltpu.make_async_remote_copy(
            src_ref=src, dst_ref=dst, send_sem=send, recv_sem=recv,
            device_id=where, device_id_type=MESH,
        )

    loads = [
        pltpu.make_async_copy(src, dst, local_sem.at[i])
        for i, (src, dst) in enumerate(
            ((x_hbm, own.at[0]), (pout_hbm, pout), (w_hbm, w), (pin_hbm, pin), (ids_hbm, ids), (h_hbm, h))
        )
    ]
    for load in loads[:2]:
        load.start()

    barrier = pltpu.get_barrier_semaphore()

    def greet(p, carry):
        pl.semaphore_signal(barrier, inc=1, device_id={"fsdp": peer(p)}, device_id_type=MESH)
        return carry

    lax.fori_loop(1, chips, greet, 0)
    pl.semaphore_signal(barrier, inc=1, device_id={"fsdp": sibling}, device_id_type=MESH)
    for k in range(1, groups):
        pl.semaphore_signal(
            barrier, inc=1, device_id={"grp": lax.rem(grp + k, groups)}, device_id_type=MESH
        )
    loads[0].wait()
    loads[1].wait()
    for load in loads[2:]:
        load.start()
    rts[core, side, along] = dot(pout[...], own[0], NT)
    pl.semaphore_wait(barrier, chips + groups - 1)

    def first(s, way):
        part_of = s % 2 if way == 0 else 1 - s % 2
        return remote(
            x_hbm.at[pl.ds(part_of * half, half)], gath.at[s, 0, way],
            ring_send.at[s, way], ring_recv.at[s, way], fsdp=right if way == 0 else left,
        )

    def onward(s, way):
        return remote(
            gath.at[s - 2, 0, way], gath.at[s, 0, way],
            ring_send.at[s, way], ring_recv.at[s, way], fsdp=right if way == 0 else left,
        )

    def across(s, way):
        return remote(
            gath.at[s, 0, way], gath.at[s, 1, way],
            sib_send.at[s, way], sib_recv.at[s, way], fsdp=sibling,
        )

    def rt_copy(p):
        mine = rts.at[core, side, along]
        return remote(mine, mine, rt_send.at[p - 1], rt_recv.at[p - 1], fsdp=peer(2 * p))

    def over_line(action):
        def step(p, carry):
            action(p)
            return carry

        lax.fori_loop(1, half_chips, step, 0)

    flip = (2 * along + 1 - side) * 2 + core
    rt_flip = remote(rts.at[core, side], rts.at[core, side], flip_send, flip_recv, fsdp=flip)
    over_line(lambda p: rt_copy(p).start())
    for s in range(min(2, steps)):
        for way in range(2):
            first(s, way).start()
    def relay(i, src, dst):
        return remote(src, dst, relay_send.at[i], relay_recv.at[i], fsdp=sibling)

    own_copy = relay(0, x_hbm, own.at[1])
    rt_relay = relay(1, rts.at[core], rts.at[core])
    part_relay = relay(2, part.at[1 - core], other)
    feats_relay = relay(3, feats.at[grp, core], feats.at[grp, core])
    own_copy.start()

    def red_copy(p):
        return remote(
            part.at[core, chip_on(p)], red.at[chip],
            red_send.at[p - 1], red_recv.at[p - 1], fsdp=peer(p),
        )

    def f_copy(p):
        mine = feats.at[grp, core, chip]
        return remote(mine, mine, f_send.at[p - 1], f_recv.at[p - 1], fsdp=peer(p))

    def x_copy(k):
        return remote(
            feats.at[grp], feats.at[grp], x_send.at[k - 1], x_recv.at[k - 1],
            grp=lax.rem(grp + k, groups),
        )

    def over_peers(action):
        def step(p, carry):
            action(p)
            return carry

        lax.fori_loop(1, chips, step, 0)

    def out_copies(unit, places):
        return [
            pltpu.make_async_copy(
                out.at[unit, pl.ds(i * half, half)],
                out_hbm.at[pl.ds(pl.multiple_of(place, half), half)],
                out_sem.at[unit, i],
            )
            for i, place in enumerate(places)
        ]

    def multiply(unit, of, block, places):
        for start in range(0, width, 256):
            stop = min(width, start + 256)
            out[unit, of * rows:(of + 1) * rows, start:stop] = dot(block, w[start:stop, :], NT).astype(out.dtype)
        for copy in out_copies(unit, places)[2 * of:2 * of + 2]:
            copy.start()

    loads[2].wait()
    own_places = (me * rows, me * rows + half, sibling * rows, sibling * rows + half)
    multiply(0, 0, own[0], own_places)
    own_copy.wait_recv()
    multiply(0, 1, own[1], own_places)
    over_line(lambda p: rt_copy(p).wait_recv())
    rt_flip.start()

    def share_right():
        rt_flip.wait_recv()
        rt_relay.start()

    def partial_feats():
        for load in loads[3:]:
            load.wait()
        rt_relay.wait_recv()
        r = lax.broadcasted_iota(jnp.int32, (PROJ, PROJ), 0)
        c = lax.broadcasted_iota(jnp.int32, (PROJ, PROJ), 1)
        mid = PROJ // 2
        odd = lax.div(r, mid)
        spot = lax.rem(r, mid)
        holder = 2 * lax.div(lax.rem(spot, mid // 2), chunks) + lax.div(spot, mid // 2)
        wanted = 2 * (holder * chunks + lax.rem(spot, chunks)) + odd
        order = jnp.where(c == wanted, 1.0, 0.0).astype(jnp.bfloat16)
        sorted_in = lax.dot_general(
            order, pin[...], (((1,), (0,)), ((), ())), preferred_element_type=jnp.float32
        ).astype(jnp.bfloat16)
        part[...] = jnp.zeros_like(part)
        which = lax.broadcasted_iota(jnp.int32, (EX_GRP, rows), 0)
        blank = jnp.zeros((PROJ, rows), jnp.bfloat16)

        def halves(a):
            high = a.astype(jnp.bfloat16)
            return high, (a - high.astype(jnp.float32)).astype(jnp.bfloat16)

        def block(b, carry):
            piece = h[pl.ds(pl.multiple_of(b * rows, rows), rows), :]
            left_t = dot(sorted_in, piece, NT)
            onehot = jnp.where(ids[b] == which, 1.0, 0.0)
            right_high, right_low = halves(
                rts[lax.rem(b, 2), lax.rem(lax.div(b, 2), 2), lax.div(b, 4)]
            )
            total = part[...].reshape(mid * EX_GRP, LANES)
            for i in range(2):
                rows_of = left_t[i * mid:(i + 1) * mid]
                weighted = (rows_of[:, None, :] * onehot[None]).reshape(mid * EX_GRP, rows)
                high, low = halves(weighted)
                for a, r in ((high, right_high), (high, right_low), (low, right_high)):
                    pair = (blank, r) if i else (r, blank)
                    total += dot(a, jnp.concatenate(pair, axis=0), NT)
            part[...] = total.reshape(part.shape)
            return carry

        lax.fori_loop(0, n, block, 0)
        part_relay.start()

    def reduce_chip():
        part_relay.wait_recv()
        part[core] = part[core] + other[...]
        over_peers(lambda p: red_copy(p).start())

    def reduce_feats():
        over_peers(lambda p: red_copy(p).wait_recv())

        def add(p, total):
            return total + red[lax.rem(chip + chips - p, chips)]

        feats[grp, core, chip] = lax.fori_loop(1, chips, add, part[core, chip]) * scale
        over_peers(lambda p: f_copy(p).start())

    def share_chip():
        over_peers(lambda p: f_copy(p).wait_recv())
        feats_relay.start()

    def share_groups():
        feats_relay.wait_recv()
        for k in range(1, groups):
            x_copy(k).start()

    gram_copy = pltpu.make_async_copy(gram, gram_hbm, gram_sem)

    def gram_block():
        for k in range(1, groups):
            x_copy(k).wait_recv()
        for q in range(n):
            for m in range(chunks):
                column = (q * chunks + m) * LANES
                piece = feats[:, q % 2, q // 2, m].reshape(examples, LANES)
                flat[:, column:column + LANES] = piece
        cols = chunks * LANES
        mine = flat[:, pl.ds(pl.multiple_of(me * cols, cols), cols)] * (1.0 / examples)
        tile = min(512, gram_rows)

        def rows_of(t, carry):
            at = pl.multiple_of(grp * gram_rows + t * tile, tile)
            gram[pl.ds(pl.multiple_of(t * tile, tile), tile), :] = dot(
                flat[:, pl.ds(at, tile)], mine, TN, HIGH
            )
            return carry

        lax.fori_loop(0, gram_rows // tile, rows_of, 0)
        gram_copy.start()

    def score():
        every = flat[...]
        matrix = dot(every, every, NT, HIGH)
        r = lax.broadcasted_iota(jnp.int32, (examples, examples), 0)
        c = lax.broadcasted_iota(jnp.int32, (examples, examples), 1)
        diagonal = jnp.where(r == c, matrix, 0.0)
        ridge = jnp.sum(jnp.sum(diagonal, axis=1, keepdims=True), axis=0, keepdims=True)
        ridge = ridge * (1.0 / examples)
        matrix = matrix + jnp.where(r == c, ridge, 0.0)
        c1 = lax.broadcasted_iota(jnp.int32, (1, examples), 1)

        def eliminate(j, a):
            row = jnp.sum(jnp.where(r == j, a, 0.0), axis=0, keepdims=True)
            col = jnp.sum(jnp.where(c == j, a, 0.0), axis=1, keepdims=True)
            pivot = jnp.sum(jnp.where(c1 == j, row, 0.0), axis=1, keepdims=True)
            row = jnp.where(c1 == j, 1.0, row) / pivot
            return jnp.where(r == j, row, jnp.where(c == j, 0.0, a) - col * row)

        inverse = lax.fori_loop(0, examples, eliminate, matrix)
        diagonal = jnp.sum(jnp.where(r == c, inverse, 0.0), axis=0, keepdims=True)
        score_ref[...] = 1.0 - ridge * diagonal

    phases = (
        (0, False, share_right), (1, True, partial_feats), (1, False, reduce_chip),
        (2, False, reduce_feats), (3, False, share_chip), (4, True, share_groups),
        (4, False, gram_block), (5, False, score),
    )

    def run_phases(s, early):
        for at, when, phase in phases:
            if steps > 5:
                if when == early:
                    pl.when(s == at)(phase)
            elif early:
                pl.when(s == min(at, steps - 1))(phase)

    def places(s):
        distance = lax.div(s, 2) + 1
        which = lax.rem(s, 2)
        found = []
        for of in (core, 1 - core):
            for way in range(2):
                at = chip_at(pos - distance if way == 0 else pos + distance)
                offset = (which if way == 0 else 1 - which) * half
                found.append((at * 2 + of) * rows + offset)
        return found

    def finish(s):
        multiply(s + 1, 0, gath[s, 0].reshape(rows, -1), places(s))
        for way in range(2):
            across(s, way).wait_recv()
        multiply(s + 1, 1, gath[s, 1].reshape(rows, -1), places(s))

    def ring(s, carry):
        for way in range(2):
            remote(
                gath.at[s, 0, way], gath.at[s, 0, way],
                ring_send.at[s, way], ring_recv.at[s, way], fsdp=right if way == 0 else left,
            ).wait_recv()

            @pl.when(s + 2 < steps)
            def _():
                onward(s + 2, way).start()

            across(s, way).start()

        run_phases(s, True)
        finish(s)
        run_phases(s, False)
        return carry

    lax.fori_loop(0, steps, ring, 0)

    def sent(s, carry):
        for way in range(2):
            across(s, way).wait_send()

        return carry

    lax.fori_loop(0, steps, sent, 0)
    for s in range(min(2, steps)):
        for way in range(2):
            first(s, way).wait_send()

    def sent_on(s, carry):
        for way in range(2):
            onward(s, way).wait_send()
        return carry

    lax.fori_loop(2, steps, sent_on, 0)
    for copy in (own_copy, rt_flip, rt_relay, part_relay, feats_relay):
        copy.wait_send()
    over_line(lambda p: rt_copy(p).wait_send())
    for copies in (red_copy, f_copy):
        over_peers(lambda p: copies(p).wait_send())
    for k in range(1, groups):
        x_copy(k).wait_send()
    gram_copy.wait()
    for copy in out_copies(0, own_places):
        copy.wait()

    def written(s, carry):
        for copy in out_copies(s + 1, places(s)):
            copy.wait()
        return carry

    lax.fori_loop(0, steps, written, 0)


def body(hidden_act, grad_output, down_weight, proj_in, proj_out, example_ids):
    n = lax.axis_size("fsdp")
    groups = lax.axis_size("grp")
    h = hidden_act[0]
    x = grad_output[0]
    rows, depth = x.shape
    tokens, width = h.shape
    chips = n // 2
    half_chips = chips // 2
    steps = chips - 1
    feat_width = PROJ * PROJ
    examples = EX_GRP * groups
    chunks = feat_width // LANES // n
    scale = (EX_GRP / tokens) ** 0.5
    ids = example_ids.reshape(n, 1, rows)
    f32, bf16 = jnp.float32, jnp.bfloat16
    dma = pltpu.SemaphoreType.DMA
    vmem = pl.BlockSpec(memory_space=pltpu.VMEM)
    hbm = pl.BlockSpec(memory_space=pl.ANY)
    pinned = pl.BlockSpec(memory_space=pltpu.HBM)
    out, gram, scores = pl.pallas_call(
        functools.partial(kernel, n, groups, scale),
        out_shape=(
            jax.ShapeDtypeStruct((tokens, width), bf16),
            jax.ShapeDtypeStruct((feat_width // groups, feat_width // n), f32),
            jax.ShapeDtypeStruct((1, examples), f32),
        ),
        in_specs=[pinned] * 6,
        out_specs=(hbm, hbm, vmem),
        scratch_shapes=[
            pltpu.VMEM((steps, 2, 2, rows // 2, depth), bf16),
            pltpu.VMEM((2, rows, depth), bf16),
            pltpu.VMEM((width, depth), bf16),
            pltpu.VMEM((tokens, width), bf16),
            pltpu.VMEM((PROJ, width), bf16),
            pltpu.VMEM((PROJ, depth), bf16),
            pltpu.VMEM((n, 1, rows), jnp.int32),
            pltpu.VMEM((2, 2, chips // 2, PROJ, rows), f32),
            pltpu.VMEM((2, chips, chunks, EX_GRP, LANES), f32),
            pltpu.VMEM((chips, chunks, EX_GRP, LANES), f32),
            pltpu.VMEM((chips, chunks, EX_GRP, LANES), f32),
            pltpu.VMEM((groups, 2, chips, chunks, EX_GRP, LANES), f32),
            pltpu.VMEM((examples, feat_width), f32),
            pltpu.VMEM((steps + 1, 2 * rows, width), bf16),
            pltpu.VMEM((feat_width // groups, feat_width // n), f32),
            dma((6,)),
            dma((steps + 1, 4)),
            dma,
            dma((steps, 2)),
            dma((steps, 2)),
            dma((steps, 2)),
            dma((steps, 2)),
            dma((4,)),
            dma((4,)),
            dma,
            dma,
            dma((half_chips - 1,)),
            dma((half_chips - 1,)),
            dma((chips - 1,)),
            dma((chips - 1,)),
            dma((max(1, groups - 1),)),
            dma((max(1, groups - 1),)),
            dma((chips - 1,)),
            dma((chips - 1,)),
        ],
        compiler_params=pltpu.CompilerParams(
            collective_id=0, has_side_effects=True, vmem_limit_bytes=44 * 1024 * 1024
        ),
        cost_estimate=pl.CostEstimate(
            flops=2 * tokens * depth * width, bytes_accessed=2 * width * (depth + 2 * tokens),
            transcendentals=0,
        ),
    )(*[
        pltpu.with_memory_space_constraint(operand, pltpu.HBM)
        for operand in (x, down_weight, h, proj_in.T, proj_out.T, ids)
    ])
    return out[None], gram, scores.reshape(examples)


def solution(mesh):
    in_specs = (
        P("grp", None, "fsdp"),
        P("grp", "fsdp", None),
        P("fsdp", None),
        P("fsdp", None),
        P(),
        P("grp", None),
    )
    out_specs = (P("grp", None, "fsdp"), P("grp", "fsdp"), P())
    return jax.shard_map(body, mesh=mesh, in_specs=in_specs, out_specs=out_specs, check_vma=False)
```
